32 devices in a mesh: groups: 2 (over x), sector: 16 (over z, y, core).
Axes of the slice: x: 2, y: 2, z: 4, core: 2. Of those that a mesh axis runs over, the one named last changes fastest.
Arguments:
- psi_blocks: bfloat16 [1024, 64, 64], P(('groups', 'sector')), parts along dimension 0
- left_sector: int32 [1024], P(('groups', 'sector')), parts along dimension 0, may hold values from 0 to 127, as said below
- left_dims: int32 [256], P(('groups', 'sector')), parts along dimension 0, may hold values from 32 to 64
- right_sector: int32 [1024], P('groups'), parts along dimension 0, may hold values from 0 to 255, as said below
- right_dims: int32 [512], P('groups'), parts along dimension 0, may hold values from 32 to 64
- left_env: bfloat16 [256, 64, 2560], P(('groups', 'sector')), parts along dimension 0
- right_env: bfloat16 [512, 64, 2560], P(('groups', 'sector')), parts along dimension 0
Outputs:
- hpsi: float32 [1024, 64, 64], P(('groups', 'sector')), parts along dimension 0
- correction: float32 [1024, 64, 64], P(('groups', 'sector')), parts along dimension 0
- theta: float32 [2], P('groups'), parts along dimension 0
The draws below stay inside these ranges and needn't reach their ends.
There are 2 independent parts, one for each index of `groups`. The reference program is written for one: setup_inputs(seed, part) draws one part's arguments, and reference() takes and returns one part's arrays. A program takes and returns all parts, laid end to end along the dimension named above; each array names one. Nothing has to cross between parts.
Inputs may be any that keep to these rules, and one draw needn't show every extreme that they name: Block g names a left sector of its own device: left_sector[g] // 8 == g // 32. `right_sector`: among the 32 blocks of one device at most 4 name right sectors of one owner (right sector s belongs to owner s // 16), and every device has an owner named by exactly 4 of its blocks. How many blocks an owner receives in all varies from owner to owner.
All inputs are finite; a program needn't handle non-finite values.
Results may differ from the reference program's by a relative error of at most 0.0047.
Values may be sent and summed in bfloat16 or wider, within the bound.
A program may use at most 192 MiB of HBM per device.

```python
import jax
import jax.numpy as jnp
from jax import lax

T_SIZE = 64
W = 40
BLK_DEV = 32
LS_DEV = 8
RS_DEV = 16
NBLK = 512
LSECT = 128
RSECT = 256
CAP = 4


def add_diagonal(noise, diag):
    eye = jnp.eye(T_SIZE, dtype=jnp.float32)
    first = (jnp.arange(W) == 0).astype(jnp.float32)
    full = noise + diag[:, :, None, None] * first[None, None, :, None] * eye[None, :, None, :]
    return full.reshape(noise.shape[0], T_SIZE, W * T_SIZE).astype(jnp.bfloat16)


def draw_right_sector(key, part):
    key = jax.random.fold_in(key, 11)
    owners = NBLK // BLK_DEV
    places = owners * CAP
    k_popular, k_devices = jax.random.split(key)
    popular = jax.random.permutation(k_popular, owners).astype(jnp.int32)

    def one_device(dev_key, device):
        k_order, k_sure, k_shuffle, k_pick = jax.random.split(dev_key, 4)
        ranks = jax.random.permutation(k_order, places).astype(jnp.int32)
        slot_owner = jnp.arange(places, dtype=jnp.int32) // CAP
        sure = (device + jax.random.randint(k_sure, (), 1, owners)) % owners
        sortkey = jnp.where(slot_owner == sure, 0, 8 * places) + ranks + 2 * CAP * popular[slot_owner]
        chosen = jnp.argsort(sortkey)[:BLK_DEV].astype(jnp.int32)
        chosen = jax.random.permutation(k_shuffle, chosen)
        owner = chosen // CAP
        return owner * RS_DEV + jax.random.randint(k_pick, (BLK_DEV,), 0, RS_DEV)
    keys = jax.random.split(k_devices, owners)
    return jax.vmap(one_device)(keys, jnp.arange(owners, dtype=jnp.int32)).reshape(NBLK).astype(jnp.int32)


def draw_left_sector(key, part):
    key = jax.random.fold_in(key, 12)
    device = jnp.arange(NBLK, dtype=jnp.int32) // BLK_DEV
    return (device * LS_DEV + jax.random.randint(key, (NBLK,), 0, LS_DEV)).astype(jnp.int32)


def draw_psi_blocks(key, part):
    left_all = draw_left_env(key, part).astype(jnp.float32)
    right_all = draw_right_env(key, part).astype(jnp.float32)
    left_ids = draw_left_sector(key, part)
    right_ids = draw_right_sector(key, part)
    key = jax.random.fold_in(key, 13)
    ramp = 1.0 + 2.0 * jnp.arange(NBLK, dtype=jnp.float32) / NBLK
    seed_blocks = jax.random.normal(key, (NBLK, T_SIZE, T_SIZE), jnp.float32)

    def apply_group(items):
        seed_part, left_part, right_part = items
        chosen_left = left_all[left_part].reshape(-1, T_SIZE, W, T_SIZE)
        partial_value = jnp.einsum('bawc,bcd->bawd', chosen_left, seed_part, precision=lax.Precision.HIGHEST)
        chosen_right = right_all[right_part].reshape(-1, T_SIZE, W, T_SIZE)
        return jnp.einsum('bawd,bewd->bae', partial_value, chosen_right, precision=lax.Precision.HIGHEST)
    applied = lax.map(apply_group, (seed_blocks.reshape(-1, BLK_DEV, T_SIZE, T_SIZE), left_ids.reshape(-1, BLK_DEV), right_ids.reshape(-1, BLK_DEV)))
    applied = applied.reshape(NBLK, T_SIZE, T_SIZE)
    return (0.6 * applied * ramp[:, None, None]).astype(jnp.bfloat16)


def draw_left_env(key, part):
    key = jax.random.fold_in(key, 14)
    k_noise, k_diag = jax.random.split(key)
    scale = (T_SIZE * W) ** (-0.5)
    noise = jax.random.normal(k_noise, (LSECT, T_SIZE, W, T_SIZE), jnp.float32) * scale
    diag = jax.random.uniform(k_diag, (LSECT, T_SIZE), jnp.float32, 0.5, 1.5)
    return add_diagonal(noise, diag)


def draw_right_env(key, part):
    key = jax.random.fold_in(key, 15)
    k_noise, k_diag = jax.random.split(key)
    scale = T_SIZE ** (-0.5)
    noise = jax.random.normal(k_noise, (RSECT, T_SIZE, W, T_SIZE), jnp.float32) * scale
    diag = jax.random.uniform(k_diag, (RSECT, T_SIZE), jnp.float32, 0.5, 1.5)
    return add_diagonal(noise, diag)


def touch_ends(values, rng, low, top_value):
    spot = [jax.random.randint(jax.random.fold_in(rng, axis), (), 0, length) for axis, length in enumerate(values.shape)]
    main_axis = values.shape.index(max(values.shape))
    next_to = spot[:main_axis] + [(spot[main_axis] + 1) % values.shape[main_axis]] + spot[main_axis + 1:]
    return values.at[tuple(spot)].set(low).at[tuple(next_to)].set(top_value)


def setup_inputs(seed: int = 0, part: int = 0) -> dict:
    arg_keys = jax.random.split(jax.random.key(seed), 8)
    part_keys = jax.random.split(jax.random.fold_in(arg_keys[7], part), 8)
    return {
        "psi_blocks": draw_psi_blocks(jax.random.fold_in(jax.random.fold_in(arg_keys[7], part), 71), part),
        "left_sector": draw_left_sector(jax.random.fold_in(jax.random.fold_in(arg_keys[7], part), 71), part),
        "left_dims": touch_ends(jax.random.randint(part_keys[2], (LSECT,), T_SIZE // 2, T_SIZE + 1), jax.random.fold_in(part_keys[2], 1), T_SIZE // 2, T_SIZE).astype(jnp.int32),
        "right_sector": draw_right_sector(jax.random.fold_in(jax.random.fold_in(arg_keys[7], part), 71), part),
        "right_dims": touch_ends(jax.random.randint(part_keys[4], (RSECT,), T_SIZE // 2, T_SIZE + 1), jax.random.fold_in(part_keys[4], 1), T_SIZE // 2, T_SIZE).astype(jnp.int32),
        "left_env": draw_left_env(jax.random.fold_in(jax.random.fold_in(arg_keys[7], part), 71), part),
        "right_env": draw_right_env(jax.random.fold_in(jax.random.fold_in(arg_keys[7], part), 71), part),
    }


def reference(psi_blocks, left_sector, left_dims, right_sector, right_dims, left_env, right_env):
    count = psi_blocks.shape[0]
    tile = psi_blocks.shape[1]
    bonds = left_env.shape[2] // tile
    rows = left_dims[left_sector]
    cols = right_dims[right_sector]
    place = jnp.arange(tile, dtype=jnp.int32)
    mask = (place[None, :, None] < rows[:, None, None]) & (place[None, None, :] < cols[:, None, None])
    psi_used = jnp.where(mask, psi_blocks, jnp.zeros_like(psi_blocks))

    def apply_group(items):
        psi_part, left_part, right_part = items
        chosen_left = left_env[left_part].reshape(-1, tile, bonds, tile).astype(jnp.float32)
        partial_value = jnp.einsum('bawc,bcd->bawd', chosen_left, psi_part.astype(jnp.float32)).astype(jnp.bfloat16)
        partial_value = lax.optimization_barrier(partial_value)
        partial_value = partial_value.reshape(-1, tile, bonds * tile).astype(jnp.float32)
        chosen_right = right_env[right_part].astype(jnp.float32)
        return jnp.einsum('bax,bex->bae', partial_value, chosen_right)
    grouped = lax.map(apply_group, (psi_used.reshape(-1, BLK_DEV, tile, tile), left_sector.reshape(-1, BLK_DEV), right_sector.reshape(-1, BLK_DEV)))
    hpsi = jnp.where(mask, grouped.reshape(count, tile, tile), jnp.float32(0.0))
    psi_float = psi_used.astype(jnp.float32)
    theta = jnp.sum(psi_float * hpsi) / jnp.sum(psi_float * psi_float)
    resid = hpsi - theta * psi_float
    spread = jnp.sum(resid * resid)
    scale = jnp.sqrt(spread / (count * tile * tile) + 1e-06)
    return (hpsi, resid / scale, jnp.reshape(theta, (1,)))
```

```python
import functools

import jax
import jax.numpy as jnp
from jax import lax
from jax.experimental import pallas as pl
from jax.experimental.pallas import tpu as pltpu
from jax.sharding import PartitionSpec as P


def apply_kernel(li, ri, pi, ok, psi_ref, l_ref, r_ref, out_ref):
    s = pl.program_id(0)
    tile = psi_ref.shape[1]
    wide = 4 * tile
    chunks = l_ref.shape[2] // wide

    @pl.when(ok[s] > 0)
    def _():
        psi = psi_ref[0]
        row = jnp.concatenate([psi] * 4, axis=1)
        full = jnp.concatenate([row] * 4, axis=0)
        ia = lax.broadcasted_iota(jnp.int32, (wide, wide), 0) // tile
        ib = lax.broadcasted_iota(jnp.int32, (wide, wide), 1) // tile
        diag = jnp.where(ia == ib, full, jnp.zeros_like(full))
        acc = jnp.zeros((tile, tile), jnp.float32)
        for k in range(chunks):
            cut = slice(k * wide, (k + 1) * wide)
            t = jnp.dot(l_ref[0, :, cut], diag, preferred_element_type=jnp.float32)
            acc += lax.dot_general(
                t.astype(jnp.bfloat16), r_ref[0, :, cut], (((1,), (1,)), ((), ())),
                preferred_element_type=jnp.float32,
            )
        out_ref[0] = acc

    @pl.when(ok[s] == 0)
    def _():
        out_ref[0] = jnp.zeros_like(out_ref[0])


def apply_blocks(li, ri, pi, ok, psi, left, right):
    slots = li.shape[0]
    tile = psi.shape[1]
    width = left.shape[2]
    return pl.pallas_call(
        apply_kernel,
        grid_spec=pltpu.PrefetchScalarGridSpec(
            num_scalar_prefetch=4,
            grid=(slots,),
            in_specs=[
                pl.BlockSpec((1, tile, tile), lambda s, li, ri, pi, ok: (pi[s], 0, 0)),
                pl.BlockSpec((1, tile, width), lambda s, li, ri, pi, ok: (li[s], 0, 0)),
                pl.BlockSpec((1, tile, width), lambda s, li, ri, pi, ok: (ri[s], 0, 0)),
            ],
            out_specs=pl.BlockSpec((1, tile, tile), lambda s, li, ri, pi, ok: (s, 0, 0)),
        ),
        out_shape=jax.ShapeDtypeStruct((slots, tile, tile), jnp.float32),
        compiler_params=pltpu.CompilerParams(vmem_limit_bytes=32 * 1024 * 1024),
    )(li, ri, pi, ok, psi, left, right)


def body(psi_blocks, left_sector, left_dims, right_sector, right_dims, left_env, right_env):
    blocks, tile = psi_blocks.shape[:2]
    left_count = left_env.shape[0]
    right_count = right_env.shape[0]
    owners = lax.axis_size("sector")
    device = lax.axis_index("sector")
    cap = (2 * blocks + owners - 1) // owners
    q = 4
    p = owners // q
    slots = min(q * cap, blocks)
    along_z = [[z * q + y for z in range(p)] for y in range(q)]
    along_y = [[z * q + y for y in range(q)] for z in range(p)]
    my_z, my_y = device // q, device % q

    left_local = left_sector - device * left_count
    table = right_sector.reshape(owners, blocks)
    own_sector = lax.dynamic_index_in_dim(table, device, 0, keepdims=False)
    rows = jnp.sum(
        jnp.where(left_local[:, None] == jnp.arange(left_count, dtype=jnp.int32)[None, :],
                  left_dims[None, :], 0), axis=1)
    cols = jnp.sum(
        jnp.where(own_sector[:, None] == jnp.arange(right_dims.shape[0], dtype=jnp.int32)[None, :],
                  right_dims[None, :], 0), axis=1)
    place = jnp.arange(tile, dtype=jnp.int32)
    mask = (place[None, :, None] < rows[:, None, None]) & (
        place[None, None, :] < cols[:, None, None])
    psi_used = jnp.where(mask, psi_blocks, jnp.zeros_like(psi_blocks))

    left_all = lax.all_gather(left_env, "sector", axis_index_groups=along_z, tiled=True)
    right_all = lax.all_gather(right_env, "sector", axis_index_groups=along_y, tiled=True)
    psi_all = lax.all_gather(psi_used, "sector", axis_index_groups=along_z, tiled=True)
    ids_all = lax.all_gather(left_local, "sector", axis_index_groups=along_z, tiled=True)

    line = lax.dynamic_index_in_dim(table.reshape(p, q, blocks), my_y, 1, keepdims=False)
    goal = line // (right_count * q)
    order = jnp.arange(blocks, dtype=jnp.int32)
    same = (goal[:, :, None] == goal[:, None, :]) & (order[None, None, :] < order[None, :, None])
    rank = jnp.sum(same.astype(jnp.int32), axis=2)
    match = (goal[:, None, :] == my_z) & (
        rank[:, None, :] == jnp.arange(slots, dtype=jnp.int32)[None, :, None])

    def pick(values):
        return jnp.sum(jnp.where(match, values, 0), axis=2).reshape(p * slots)

    ok = pick(jnp.ones((p, 1, blocks), jnp.int32))
    base = jnp.arange(p, dtype=jnp.int32)[:, None, None]
    pi = pick(base * blocks + order[None, None, :])
    li = pick(base * left_count + ids_all.reshape(p, 1, blocks))
    ri = pick(line[:, None, :] - my_z * (q * right_count))
    out = apply_blocks(li, ri, pi, ok, psi_all, left_all, right_all)
    back = lax.all_to_all(out, "sector", split_axis=0, concat_axis=0, tiled=True,
                          axis_index_groups=along_z)
    own_rank = lax.dynamic_index_in_dim(rank, my_z, 0, keepdims=False)
    target = (own_sector // (right_count * q)) * slots + own_rank
    hpsi = jnp.where(mask, jnp.take(back, target, axis=0), jnp.float32(0.0))

    psi_float = psi_used.astype(jnp.float32)
    ph = jnp.sum(psi_float * hpsi)
    pp = jnp.sum(psi_float * psi_float)
    local = jnp.where(pp > 0, ph / jnp.where(pp > 0, pp, 1.0), 0.0)
    rest = hpsi - local * psi_float
    ss = jnp.sum(rest * rest)
    sums = lax.all_gather(jnp.stack([ph, pp, ss, local]), "sector")
    theta = jnp.sum(sums[:, 0]) / jnp.sum(sums[:, 1])
    gap = sums[:, 3] - theta
    spread = jnp.sum(sums[:, 2] + gap * gap * sums[:, 1])
    resid = hpsi - theta * psi_float
    scale = jnp.sqrt(spread / (blocks * owners * tile * tile) + 1e-06)
    return (hpsi, resid / scale, jnp.reshape(theta, (1,)))


def solution(mesh):
    placed = (
        P(("groups", "sector"), None, None),
        P(("groups", "sector")),
        P(("groups", "sector")),
        P("groups"),
        P("groups"),
        P(("groups", "sector"), None, None),
        P(("groups", "sector"), None, None),
    )
    return jax.shard_map(
        body,
        mesh=mesh,
        in_specs=placed,
        out_specs=(
            P(("groups", "sector"), None, None),
            P(("groups", "sector"), None, None),
            P("groups"),
        ),
        check_vma=False,
    )
```

```python
import functools

import jax
import jax.numpy as jnp
from jax import lax
from jax.experimental import pallas as pl
from jax.experimental.pallas import tpu as pltpu
from jax.sharding import PartitionSpec as P


def peer(index):
    return dict(device_id={"sector": index}, device_id_type=pl.DeviceIdType.MESH)


def gather_kernel(p, q, chunks, left, right, psi, left_all, right_all, psi_all,
                  l_send, l_recv, s_send, s_recv, r_send, r_recv, own_sem):
    device = lax.axis_index("sector")
    z, y = device // q, device % q
    mate = z * q + (y // 2) * 2 + (1 - y % 2)
    across = z * q + (y + 2) % q
    across_y = (y + 2) % q
    n = left.shape[0] // chunks
    rights = right.shape[0]
    has_up, has_down = z + 1 < p, z > 0

    barrier = pltpu.get_barrier_semaphore()
    pl.semaphore_signal(barrier, inc=1, **peer(mate))
    pl.semaphore_signal(barrier, inc=1, **peer(across))

    @pl.when(has_up)
    def _():
        pl.semaphore_signal(barrier, inc=1, **peer(device + q))

    @pl.when(has_down)
    def _():
        pl.semaphore_signal(barrier, inc=1, **peer(device - q))

    pl.semaphore_wait(barrier, 4 - (z + 1) // p - (p - z) // p)

    own = [
        pltpu.make_async_copy(left, left_all.at[z], own_sem.at[0]),
        pltpu.make_async_copy(right, right_all.at[y], own_sem.at[1]),
        pltpu.make_async_copy(psi, psi_all.at[z], own_sem.at[2]),
    ]

    def l_copy(way, t, c, shard):
        part = pl.ds(c * n, n)
        src = left.at[part] if t == 0 else left_all.at[shard, part]
        return pltpu.make_async_remote_copy(
            src, left_all.at[shard, part], l_send.at[way, t, c], l_recv.at[way, t, c],
            **peer(device + (q if way == 0 else -q)))

    def s_copy(way, t, shard):
        src = psi if t == 0 else psi_all.at[shard]
        return pltpu.make_async_remote_copy(
            src, psi_all.at[shard], s_send.at[way, t], s_recv.at[way, t],
            **peer(device + (q if way == 0 else -q)))

    def out_shard(way, t):
        return z - t if way == 0 else z + t

    def sends(way, t):
        return ((z - t >= 0) & has_up) if way == 0 else ((z + t < p) & has_down)

    def in_shard(way, t):
        return z - 1 - t if way == 0 else z + 1 + t

    def gets(way, t):
        return (z - 1 - t >= 0) if way == 0 else (z + 1 + t < p)

    def r_copy(kind, c):
        if kind == 0:
            src, dst, to = right.at[c], right_all.at[y, c], across
        elif kind == 1:
            src, dst, to = right.at[c], right_all.at[y, c], mate
        else:
            src, dst, to = right_all.at[across_y, c], right_all.at[across_y, c], mate
        return pltpu.make_async_remote_copy(
            src, dst, r_send.at[kind, c], r_recv.at[kind, c], **peer(to))

    def r_forward(c):
        r_copy(0, c).wait_recv()
        r_copy(2, c).start()

    merged = p > 3 and 2 * chunks == rights

    for t in range(p):
        if t < p - 1:
            for way in (0, 1):
                if t > 0:
                    @pl.when(gets(way, t - 1))
                    def _(way=way, t=t):
                        s_copy(way, t - 1, in_shard(way, t - 1)).wait_recv()

                @pl.when(sends(way, t))
                def _(way=way, t=t):
                    s_copy(way, t, out_shard(way, t)).start()

        def step(c, carry, t=t):
            for way in (0, 1):
                if t > 0:
                    @pl.when(gets(way, t - 1))
                    def _(way=way):
                        l_copy(way, t - 1, c, in_shard(way, t - 1)).wait_recv()

                if t < p - 1:
                    @pl.when(sends(way, t))
                    def _(way=way):
                        l_copy(way, t, c, out_shard(way, t)).start()
            if t in (1, 2) and merged:
                r_forward((t - 1) * chunks + c)
            return carry

        lax.fori_loop(0, chunks, step, 0)
        if t == 0:
            def first(c, carry):
                r_copy(0, c).start()
                r_copy(1, c).start()
                return carry

            lax.fori_loop(0, rights, first, 0)
            for copy in own:
                copy.start()

    for way in (0, 1):
        @pl.when(gets(way, p - 2))
        def _(way=way):
            s_copy(way, p - 2, in_shard(way, p - 2)).wait_recv()

    if not merged:
        def rest(c, carry):
            r_forward(c)
            return carry

        lax.fori_loop(0, rights, rest, 0)

    def finish(c, carry):
        r_copy(0, c).wait_send()
        r_copy(1, c).wait_send()
        r_copy(2, c).wait_send()
        r_copy(1, c).wait_recv()
        r_copy(2, c).wait_recv()
        return carry

    lax.fori_loop(0, rights, finish, 0)
    for t in range(p - 1):
        for way in (0, 1):
            @pl.when(sends(way, t))
            def _(way=way, t=t):
                s_copy(way, t, out_shard(way, t)).wait_send()

                def drain(c, carry):
                    l_copy(way, t, c, out_shard(way, t)).wait_send()
                    return carry

                lax.fori_loop(0, chunks, drain, 0)
    for copy in own:
        copy.wait()


def gather(p, q, left, right, psi):
    chunks = left.shape[0] if p <= 4 else 2
    anyspace = pl.BlockSpec(memory_space=pl.ANY)
    dma = pltpu.SemaphoreType.DMA
    return pl.pallas_call(
        functools.partial(gather_kernel, p, q, chunks),
        out_shape=(
            jax.ShapeDtypeStruct((p,) + left.shape, left.dtype),
            jax.ShapeDtypeStruct((q,) + right.shape, right.dtype),
            jax.ShapeDtypeStruct((p,) + psi.shape, psi.dtype),
        ),
        in_specs=[anyspace] * 3,
        out_specs=(anyspace,) * 3,
        scratch_shapes=[
            dma((2, p - 1, chunks)), dma((2, p - 1, chunks)),
            dma((2, p - 1)), dma((2, p - 1)),
            dma((3, right.shape[0])), dma((3, right.shape[0])), dma((3,)),
        ],
        compiler_params=pltpu.CompilerParams(collective_id=0, has_side_effects=True),
    )(left, right, psi)


def return_kernel(p, q, out, stat, back, stat_all, send, recv, st_send, st_recv, own_sem):
    device = lax.axis_index("sector")
    owners = p * q
    z, y = device // q, device % q
    barrier = pltpu.get_barrier_semaphore()

    def greet(d, carry):
        pl.semaphore_signal(barrier, inc=1, **peer((device + d) % owners))
        return carry

    lax.fori_loop(1, owners, greet, 0)
    pl.semaphore_wait(barrier, owners - 1)

    def tiles(d):
        to = (z + d) % p
        return pltpu.make_async_remote_copy(
            out.at[to], back.at[z], send.at[d], recv.at[d], **peer(to * q + y))

    def stats(d):
        return pltpu.make_async_remote_copy(
            stat, stat_all.at[device], st_send.at[d], st_recv.at[d],
            **peer((device + d) % owners))

    def each(low, high, act):
        def step(d, carry):
            act(d)
            return carry

        lax.fori_loop(low, high, step, 0)

    own = [
        pltpu.make_async_copy(out.at[z], back.at[z], own_sem.at[0]),
        pltpu.make_async_copy(stat, stat_all.at[device], own_sem.at[1]),
    ]
    each(1, owners, lambda d: stats(d).start())
    each(1, p, lambda d: tiles(d).start())
    for copy in own:
        copy.start()
    each(1, owners, lambda d: stats(d).wait())
    each(1, p, lambda d: tiles(d).wait())
    for copy in own:
        copy.wait()


def give_back(p, q, out, stat):
    anyspace = pl.BlockSpec(memory_space=pl.ANY)
    dma = pltpu.SemaphoreType.DMA
    return pl.pallas_call(
        functools.partial(return_kernel, p, q),
        out_shape=(
            jax.ShapeDtypeStruct(out.shape, out.dtype),
            jax.ShapeDtypeStruct((p * q,) + stat.shape, stat.dtype),
        ),
        in_specs=[anyspace] * 2,
        out_specs=(anyspace,) * 2,
        scratch_shapes=[dma((p,)), dma((p,)), dma((p * q,)), dma((p * q,)), dma((2,))],
        compiler_params=pltpu.CompilerParams(collective_id=1, has_side_effects=True),
    )(out, stat)


def apply_kernel(li, ri, pi, ok, rows, cols, psi0, psi1, l0, l1, r0, r1, out_ref, stat_ref):
    step = pl.program_id(0)
    tile = l0.shape[1]
    wide = 4 * tile
    chunks = l0.shape[2] // wide
    for half, (psi_ref, l_ref, r_ref) in enumerate(((psi0, l0, r0), (psi1, l1, r1))):
        s = step * 2 + half
        lanes = slice(half * tile, (half + 1) * tile)

        @pl.when(ok[s] > 0)
        def _():
            pair = psi_ref[0].astype(jnp.float32)
            psi_f = jnp.where(pi[s] % 2 == 0, pair[:, :tile], pair[:, tile:])
            psi = psi_f.astype(jnp.bfloat16)
            row = jnp.concatenate([psi] * 4, axis=1)
            full = jnp.concatenate([row] * 4, axis=0)
            ia = lax.broadcasted_iota(jnp.int32, (wide, wide), 0) // tile
            ib = lax.broadcasted_iota(jnp.int32, (wide, wide), 1) // tile
            diag = jnp.where(ia == ib, full, jnp.zeros_like(full))
            acc = jnp.zeros((tile, tile), jnp.float32)
            for k in range(chunks):
                cut = slice(k * wide, (k + 1) * wide)
                t = jnp.dot(l_ref[0, :, cut], diag, preferred_element_type=jnp.float32)
                acc += lax.dot_general(
                    t.astype(jnp.bfloat16), r_ref[0, :, cut], (((1,), (1,)), ((), ())),
                    preferred_element_type=jnp.float32,
                )
            a = lax.broadcasted_iota(jnp.int32, (tile, tile), 0)
            e = lax.broadcasted_iota(jnp.int32, (tile, tile), 1)
            acc = jnp.where((a < rows[s]) & (e < cols[s]), acc, 0.0)
            out_ref[0, :, lanes] = acc
            ph = jnp.sum(psi_f * acc, keepdims=True)
            pp = jnp.sum(psi_f * psi_f, keepdims=True)
            th = jnp.where(pp > 0, ph / jnp.where(pp > 0, pp, 1.0), 0.0)
            rest = acc - th * psi_f
            ss = jnp.sum(rest * rest, keepdims=True)
            lane = lax.broadcasted_iota(jnp.int32, (4, 128), 1)
            stat_ref[0, 4 * half:4 * half + 4, :] = jnp.where(
                lane == 0, ph, jnp.where(lane == 1, pp, jnp.where(lane == 2, ss, th)))

        @pl.when(ok[s] == 0)
        def _():
            out_ref[0, :, lanes] = jnp.zeros((tile, tile), jnp.float32)
            stat_ref[0, 4 * half:4 * half + 4, :] = jnp.zeros((4, 128), jnp.float32)


def apply_blocks(li, ri, pi, ok, rows, cols, psi, left, right):
    pairs = li.shape[0] // 2
    tile = left.shape[1]
    width = left.shape[2]

    def spec(shape, which, half, scale=1):
        return pl.BlockSpec((1,) + shape, lambda j, *ids: (ids[which][2 * j + half] // scale, 0, 0))

    return pl.pallas_call(
        apply_kernel,
        grid_spec=pltpu.PrefetchScalarGridSpec(
            num_scalar_prefetch=6,
            grid=(pairs,),
            in_specs=[
                spec((tile, 2 * tile), 2, 0, 2), spec((tile, 2 * tile), 2, 1, 2),
                spec((tile, width), 0, 0), spec((tile, width), 0, 1),
                spec((tile, width), 1, 0), spec((tile, width), 1, 1),
            ],
            out_specs=[
                pl.BlockSpec((1, tile, 2 * tile), lambda j, *ids: (j, 0, 0)),
                pl.BlockSpec((1, 8, 128), lambda j, *ids: (j, 0, 0)),
            ],
        ),
        out_shape=[
            jax.ShapeDtypeStruct((pairs, tile, 2 * tile), jnp.float32),
            jax.ShapeDtypeStruct((pairs, 8, 128), jnp.float32),
        ],
        compiler_params=pltpu.CompilerParams(vmem_limit_bytes=32 * 1024 * 1024),
    )(li, ri, pi, ok, rows, cols, psi, psi, left, left, right, right)


def body(psi_blocks, left_sector, left_dims, right_sector, right_dims, left_env, right_env):
    blocks, tile = psi_blocks.shape[:2]
    left_count = left_env.shape[0]
    right_count = right_env.shape[0]
    owners = lax.axis_size("sector")
    device = lax.axis_index("sector")
    cap = (2 * blocks + owners - 1) // owners
    q = 4
    p = owners // q
    slots = min(q * cap, blocks)
    my_z, my_y = device // q, device % q

    left_local = left_sector - device * left_count
    table = right_sector.reshape(owners, blocks)
    own_sector = lax.dynamic_index_in_dim(table, device, 0, keepdims=False)
    rows = jnp.sum(
        jnp.where(left_local[:, None] == jnp.arange(left_count, dtype=jnp.int32)[None, :],
                  left_dims[None, :], 0), axis=1)
    cols = jnp.sum(
        jnp.where(own_sector[:, None] == jnp.arange(right_dims.shape[0], dtype=jnp.int32)[None, :],
                  right_dims[None, :], 0), axis=1)
    place = jnp.arange(tile, dtype=jnp.int32)
    mask = (place[None, :, None] < rows[:, None, None]) & (
        place[None, None, :] < cols[:, None, None])
    psi_used = jnp.where(mask, psi_blocks, jnp.zeros_like(psi_blocks))
    half = blocks // 2
    packed = psi_used.reshape(half, 2, tile, tile).transpose(0, 2, 1, 3).reshape(half, tile, 2 * tile)
    extra = jnp.pad(jnp.stack([left_local, rows]).astype(jnp.bfloat16),
                    ((0, tile - 2), (0, 2 * tile - blocks)))
    sent = jnp.concatenate([packed, extra[None]], axis=0)

    left_all, right_all, psi_all = gather(p, q, left_env, right_env, sent)
    notes = psi_all[:, half, :2, :blocks].astype(jnp.int32)
    left_all = left_all.reshape(p * left_count, tile, -1)
    right_all = right_all.reshape(q * right_count, tile, -1)
    psi_all = psi_all.reshape(p * (half + 1), tile, 2 * tile)

    line = lax.dynamic_index_in_dim(table.reshape(p, q, blocks), my_y, 1, keepdims=False)
    goal = line // (right_count * q)
    order = jnp.arange(blocks, dtype=jnp.int32)
    same = (goal[:, :, None] == goal[:, None, :]) & (order[None, None, :] < order[None, :, None])
    rank = jnp.sum(same.astype(jnp.int32), axis=2)
    match = (goal[:, None, :] == my_z) & (
        rank[:, None, :] == jnp.arange(slots, dtype=jnp.int32)[None, :, None])

    def pick(values):
        return jnp.sum(jnp.where(match, values, 0), axis=2).reshape(p * slots)

    ok = pick(jnp.ones((p, 1, blocks), jnp.int32))
    base = jnp.arange(p, dtype=jnp.int32)[:, None, None]
    pi = pick(base * (blocks + 2) + order[None, None, :])
    li = pick(base * left_count + notes[:, :1])
    slot_rows = pick(notes[:, 1:])
    local_right = line[:, None, :] - my_z * (q * right_count)
    ri = pick(local_right)
    my_dims = lax.dynamic_slice_in_dim(right_dims, my_z * (q * right_count), q * right_count)
    slot_cols = jnp.sum(
        jnp.where(ri[:, None] == jnp.arange(q * right_count, dtype=jnp.int32)[None, :],
                  my_dims[None, :], 0), axis=1)
    out, stat = apply_blocks(li, ri, pi, ok, slot_rows, slot_cols, psi_all, left_all, right_all)
    wide = -(-(p * slots) // 128) * 128
    stat = stat.reshape(p * slots, 4, 128)[:, 0, :4]
    stat = jnp.pad(stat.T, ((0, 4), (0, wide - p * slots)))
    back, stat_all = give_back(p, q, out.reshape(p, slots // 2, tile, 2 * tile), stat)

    own_rank = lax.dynamic_index_in_dim(rank, my_z, 0, keepdims=False)
    target = (own_sector // (right_count * q)) * slots + own_rank
    got = jnp.take(back.reshape(p * slots // 2, tile, 2 * tile), target // 2, axis=0)
    got = jnp.where((target % 2 == 0)[:, None, None], got[:, :, :tile], got[:, :, tile:])
    hpsi = jnp.where(mask, got, jnp.float32(0.0))

    psi_float = psi_used.astype(jnp.float32)
    theta = jnp.sum(stat_all[:, 0]) / jnp.sum(stat_all[:, 1])
    gap = stat_all[:, 3] - theta
    spread = jnp.sum(stat_all[:, 2] + gap * gap * stat_all[:, 1])
    resid = hpsi - theta * psi_float
    scale = jnp.sqrt(spread / (blocks * owners * tile * tile) + 1e-06)
    return (hpsi, resid / scale, jnp.reshape(theta, (1,)))


def solution(mesh):
    placed = (
        P(("groups", "sector"), None, None),
        P(("groups", "sector")),
        P(("groups", "sector")),
        P("groups"),
        P("groups"),
        P(("groups", "sector"), None, None),
        P(("groups", "sector"), None, None),
    )
    return jax.shard_map(
        body,
        mesh=mesh,
        in_specs=placed,
        out_specs=(
            P(("groups", "sector"), None, None),
            P(("groups", "sector"), None, None),
            P("groups"),
        ),
        check_vma=False,
    )
```

```python
import functools

import jax
import jax.numpy as jnp
from jax import lax
from jax.experimental import pallas as pl
from jax.experimental.pallas import tpu as pltpu
from jax.sharding import PartitionSpec as P


def peer(index):
    return dict(device_id={"sector": index}, device_id_type=pl.DeviceIdType.MESH)


def gather_kernel(p, q, chunks, left, right, psi, left_all, right_all, psi_all,
                  l_send, l_recv, s_send, s_recv, r_send, r_recv, own_sem):
    device = lax.axis_index("sector")
    z, y = device // q, device % q
    mate = z * q + (y // 2) * 2 + (1 - y % 2)
    across = z * q + (y + 2) % q
    across_y = (y + 2) % q
    n = left.shape[0] // chunks
    rights = right.shape[0]
    has_up, has_down = z + 1 < p, z > 0

    barrier = pltpu.get_barrier_semaphore()
    pl.semaphore_signal(barrier, inc=1, **peer(mate))
    pl.semaphore_signal(barrier, inc=1, **peer(across))

    @pl.when(has_up)
    def _():
        pl.semaphore_signal(barrier, inc=1, **peer(device + q))

    @pl.when(has_down)
    def _():
        pl.semaphore_signal(barrier, inc=1, **peer(device - q))

    pl.semaphore_wait(barrier, 4 - (z + 1) // p - (p - z) // p)

    own = [
        pltpu.make_async_copy(left, left_all.at[z], own_sem.at[0]),
        pltpu.make_async_copy(right, right_all.at[y], own_sem.at[1]),
        pltpu.make_async_copy(psi, psi_all.at[z], own_sem.at[2]),
    ]

    def l_copy(way, t, c, shard):
        part = pl.ds(c * n, n)
        src = left.at[part] if t == 0 else left_all.at[shard, part]
        return pltpu.make_async_remote_copy(
            src, left_all.at[shard, part], l_send.at[way, t, c], l_recv.at[way, t, c],
            **peer(device + (q if way == 0 else -q)))

    def s_copy(way, t, shard):
        src = psi if t == 0 else psi_all.at[shard]
        return pltpu.make_async_remote_copy(
            src, psi_all.at[shard], s_send.at[way, t], s_recv.at[way, t],
            **peer(device + (q if way == 0 else -q)))

    def out_shard(way, t):
        return z - t if way == 0 else z + t

    def sends(way, t):
        return ((z - t >= 0) & has_up) if way == 0 else ((z + t < p) & has_down)

    def in_shard(way, t):
        return z - 1 - t if way == 0 else z + 1 + t

    def gets(way, t):
        return (z - 1 - t >= 0) if way == 0 else (z + 1 + t < p)

    def r_copy(kind, c):
        if kind == 0:
            src, dst, to = right.at[c], right_all.at[y, c], across
        elif kind == 1:
            src, dst, to = right.at[c], right_all.at[y, c], mate
        else:
            src, dst, to = right_all.at[across_y, c], right_all.at[across_y, c], mate
        return pltpu.make_async_remote_copy(
            src, dst, r_send.at[kind, c], r_recv.at[kind, c], **peer(to))

    def r_forward(c):
        r_copy(0, c).wait_recv()
        r_copy(2, c).start()

    merged = p > 3 and 2 * chunks == rights

    for t in range(p):
        if t < p - 1:
            for way in (0, 1):
                if t > 0:
                    @pl.when(gets(way, t - 1))
                    def _(way=way, t=t):
                        s_copy(way, t - 1, in_shard(way, t - 1)).wait_recv()

                @pl.when(sends(way, t))
                def _(way=way, t=t):
                    s_copy(way, t, out_shard(way, t)).start()

        def step(c, carry, t=t):
            for way in (0, 1):
                if t > 0:
                    @pl.when(gets(way, t - 1))
                    def _(way=way):
                        l_copy(way, t - 1, c, in_shard(way, t - 1)).wait_recv()

                if t < p - 1:
                    @pl.when(sends(way, t))
                    def _(way=way):
                        l_copy(way, t, c, out_shard(way, t)).start()
            if merged and t < 2:
                r_copy(0, t * chunks + c).start()
                r_copy(1, t * chunks + c).start()
            if merged and t in (1, 2):
                r_forward((t - 1) * chunks + c)
            return carry

        lax.fori_loop(0, chunks, step, 0)
        if t == 0:
            if not merged:
                def first(c, carry):
                    r_copy(0, c).start()
                    r_copy(1, c).start()
                    return carry

                lax.fori_loop(0, rights, first, 0)
            for copy in own:
                copy.start()

    for way in (0, 1):
        @pl.when(gets(way, p - 2))
        def _(way=way):
            s_copy(way, p - 2, in_shard(way, p - 2)).wait_recv()

    if not merged:
        def rest(c, carry):
            r_forward(c)
            return carry

        lax.fori_loop(0, rights, rest, 0)

    def finish(c, carry):
        r_copy(0, c).wait_send()
        r_copy(1, c).wait_send()
        r_copy(2, c).wait_send()
        r_copy(1, c).wait_recv()
        r_copy(2, c).wait_recv()
        return carry

    lax.fori_loop(0, rights, finish, 0)
    for t in range(p - 1):
        for way in (0, 1):
            @pl.when(sends(way, t))
            def _(way=way, t=t):
                s_copy(way, t, out_shard(way, t)).wait_send()

                def drain(c, carry):
                    l_copy(way, t, c, out_shard(way, t)).wait_send()
                    return carry

                lax.fori_loop(0, chunks, drain, 0)
    for copy in own:
        copy.wait()


def gather(p, q, left, right, psi):
    chunks = left.shape[0] if p <= 4 else 2
    anyspace = pl.BlockSpec(memory_space=pl.ANY)
    dma = pltpu.SemaphoreType.DMA
    return pl.pallas_call(
        functools.partial(gather_kernel, p, q, chunks),
        out_shape=(
            jax.ShapeDtypeStruct((p,) + left.shape, left.dtype),
            jax.ShapeDtypeStruct((q,) + right.shape, right.dtype),
            jax.ShapeDtypeStruct((p,) + psi.shape, psi.dtype),
        ),
        in_specs=[anyspace] * 3,
        out_specs=(anyspace,) * 3,
        scratch_shapes=[
            dma((2, p - 1, chunks)), dma((2, p - 1, chunks)),
            dma((2, p - 1)), dma((2, p - 1)),
            dma((3, right.shape[0])), dma((3, right.shape[0])), dma((3,)),
        ],
        compiler_params=pltpu.CompilerParams(collective_id=0, has_side_effects=True),
    )(left, right, psi)


def return_kernel(p, q, out, stat, back, stat_all, send, recv, st_send, st_recv, own_sem):
    device = lax.axis_index("sector")
    owners = p * q
    z, y = device // q, device % q
    barrier = pltpu.get_barrier_semaphore()

    def greet(d, carry):
        pl.semaphore_signal(barrier, inc=1, **peer((device + d) % owners))
        return carry

    lax.fori_loop(1, owners, greet, 0)
    pl.semaphore_wait(barrier, owners - 1)

    def tiles(d):
        to = (z + d) % p
        return pltpu.make_async_remote_copy(
            out.at[to], back.at[z], send.at[d], recv.at[d], **peer(to * q + y))

    def stats(d):
        return pltpu.make_async_remote_copy(
            stat, stat_all.at[device], st_send.at[d], st_recv.at[d],
            **peer((device + d) % owners))

    def each(low, high, act):
        def step(d, carry):
            act(d)
            return carry

        lax.fori_loop(low, high, step, 0)

    own = [
        pltpu.make_async_copy(out.at[z], back.at[z], own_sem.at[0]),
        pltpu.make_async_copy(stat, stat_all.at[device], own_sem.at[1]),
    ]
    each(1, owners, lambda d: stats(d).start())
    each(1, p, lambda d: tiles(d).start())
    for copy in own:
        copy.start()
    each(1, owners, lambda d: stats(d).wait())
    each(1, p, lambda d: tiles(d).wait())
    for copy in own:
        copy.wait()


def give_back(p, q, out, stat):
    anyspace = pl.BlockSpec(memory_space=pl.ANY)
    dma = pltpu.SemaphoreType.DMA
    return pl.pallas_call(
        functools.partial(return_kernel, p, q),
        out_shape=(
            jax.ShapeDtypeStruct(out.shape, out.dtype),
            jax.ShapeDtypeStruct((p * q,) + stat.shape, stat.dtype),
        ),
        in_specs=[anyspace] * 2,
        out_specs=(anyspace,) * 2,
        scratch_shapes=[dma((p,)), dma((p,)), dma((p * q,)), dma((p * q,)), dma((2,))],
        compiler_params=pltpu.CompilerParams(collective_id=1, has_side_effects=True),
    )(out, stat)


def apply_kernel(li, ri, pi, ok, rows, cols, psi0, psi1, l0, l1, r0, r1, out_ref, stat_ref):
    step = pl.program_id(0)
    tile = l0.shape[1]
    wide = 4 * tile
    chunks = l0.shape[2] // wide
    for half, (psi_ref, l_ref, r_ref) in enumerate(((psi0, l0, r0), (psi1, l1, r1))):
        s = step * 2 + half
        lanes = slice(half * tile, (half + 1) * tile)

        @pl.when(ok[s] > 0)
        def _():
            pair = psi_ref[0].astype(jnp.float32)
            psi_f = jnp.where(pi[s] % 2 == 0, pair[:, :tile], pair[:, tile:])
            psi = psi_f.astype(jnp.bfloat16)
            row = jnp.concatenate([psi] * 4, axis=1)
            full = jnp.concatenate([row] * 4, axis=0)
            ia = lax.broadcasted_iota(jnp.int32, (wide, wide), 0) // tile
            ib = lax.broadcasted_iota(jnp.int32, (wide, wide), 1) // tile
            diag = jnp.where(ia == ib, full, jnp.zeros_like(full))
            acc = jnp.zeros((tile, tile), jnp.float32)
            for k in range(chunks):
                cut = slice(k * wide, (k + 1) * wide)
                t = jnp.dot(l_ref[0, :, cut], diag, preferred_element_type=jnp.float32)
                acc += lax.dot_general(
                    t.astype(jnp.bfloat16), r_ref[0, :, cut], (((1,), (1,)), ((), ())),
                    preferred_element_type=jnp.float32,
                )
            a = lax.broadcasted_iota(jnp.int32, (tile, tile), 0)
            e = lax.broadcasted_iota(jnp.int32, (tile, tile), 1)
            acc = jnp.where((a < rows[s]) & (e < cols[s]), acc, 0.0)
            out_ref[0, :, lanes] = acc
            ph = jnp.sum(psi_f * acc, axis=0, keepdims=True)
            pp = jnp.sum(psi_f * psi_f, axis=0, keepdims=True)
            th = jnp.where(pp > 0, ph / jnp.where(pp > 0, pp, 1.0), 0.0)
            rest = acc - th * psi_f
            ss = jnp.sum(rest * rest, axis=0, keepdims=True)
            stat_ref[0, 0:1, lanes] = ph
            stat_ref[0, 1:2, lanes] = pp
            stat_ref[0, 2:3, lanes] = ss
            stat_ref[0, 3:4, lanes] = th

        @pl.when(ok[s] == 0)
        def _():
            out_ref[0, :, lanes] = jnp.zeros((tile, tile), jnp.float32)
            stat_ref[0, 0:4, lanes] = jnp.zeros((4, tile), jnp.float32)


def apply_blocks(li, ri, pi, ok, rows, cols, psi, left, right):
    pairs = li.shape[0] // 2
    tile = left.shape[1]
    width = left.shape[2]

    def spec(shape, which, half, scale=1):
        return pl.BlockSpec((1,) + shape, lambda j, *ids: (ids[which][2 * j + half] // scale, 0, 0))

    return pl.pallas_call(
        apply_kernel,
        grid_spec=pltpu.PrefetchScalarGridSpec(
            num_scalar_prefetch=6,
            grid=(pairs,),
            in_specs=[
                spec((tile, 2 * tile), 2, 0, 2), spec((tile, 2 * tile), 2, 1, 2),
                spec((tile, width), 0, 0), spec((tile, width), 0, 1),
                spec((tile, width), 1, 0), spec((tile, width), 1, 1),
            ],
            out_specs=[
                pl.BlockSpec((1, tile, 2 * tile), lambda j, *ids: (j, 0, 0)),
                pl.BlockSpec((1, 4, 2 * tile), lambda j, *ids: (j, 0, 0)),
            ],
        ),
        out_shape=[
            jax.ShapeDtypeStruct((pairs, tile, 2 * tile), jnp.float32),
            jax.ShapeDtypeStruct((pairs, 4, 2 * tile), jnp.float32),
        ],
        compiler_params=pltpu.CompilerParams(vmem_limit_bytes=56 * 1024 * 1024),
    )(li, ri, pi, ok, rows, cols, psi, psi, left, left, right, right)


def body(psi_blocks, left_sector, left_dims, right_sector, right_dims, left_env, right_env):
    blocks, tile = psi_blocks.shape[:2]
    left_count = left_env.shape[0]
    right_count = right_env.shape[0]
    owners = lax.axis_size("sector")
    device = lax.axis_index("sector")
    cap = (2 * blocks + owners - 1) // owners
    q = 4
    p = owners // q
    slots = min(q * cap, blocks)
    my_z, my_y = device // q, device % q

    left_local = left_sector - device * left_count
    table = right_sector.reshape(owners, blocks)
    own_sector = lax.dynamic_index_in_dim(table, device, 0, keepdims=False)
    rows = jnp.sum(
        jnp.where(left_local[:, None] == jnp.arange(left_count, dtype=jnp.int32)[None, :],
                  left_dims[None, :], 0), axis=1)
    cols = jnp.sum(
        jnp.where(own_sector[:, None] == jnp.arange(right_dims.shape[0], dtype=jnp.int32)[None, :],
                  right_dims[None, :], 0), axis=1)
    place = jnp.arange(tile, dtype=jnp.int32)
    mask = (place[None, :, None] < rows[:, None, None]) & (
        place[None, None, :] < cols[:, None, None])
    psi_used = jnp.where(mask, psi_blocks, jnp.zeros_like(psi_blocks))
    half = blocks // 2
    packed = psi_used.reshape(half, 2, tile, tile).transpose(0, 2, 1, 3).reshape(half, tile, 2 * tile)
    extra = jnp.pad(jnp.stack([left_local, rows]).astype(jnp.bfloat16),
                    ((0, tile - 2), (0, 2 * tile - blocks)))
    sent = jnp.concatenate([packed, extra[None]], axis=0)

    left_all, right_all, psi_all = gather(p, q, left_env, right_env, sent)
    notes = psi_all[:, half, :2, :blocks].astype(jnp.int32)
    left_all = left_all.reshape(p * left_count, tile, -1)
    right_all = right_all.reshape(q * right_count, tile, -1)
    psi_all = psi_all.reshape(p * (half + 1), tile, 2 * tile)

    line = lax.dynamic_index_in_dim(table.reshape(p, q, blocks), my_y, 1, keepdims=False)
    goal = line // (right_count * q)
    order = jnp.arange(blocks, dtype=jnp.int32)
    same = (goal[:, :, None] == goal[:, None, :]) & (order[None, None, :] < order[None, :, None])
    rank = jnp.sum(same.astype(jnp.int32), axis=2)
    match = (goal[:, None, :] == my_z) & (
        rank[:, None, :] == jnp.arange(slots, dtype=jnp.int32)[None, :, None])

    def pick(values):
        return jnp.sum(jnp.where(match, values, 0), axis=2).reshape(p * slots)

    ok = pick(jnp.ones((p, 1, blocks), jnp.int32))
    base = jnp.arange(p, dtype=jnp.int32)[:, None, None]
    pi = pick(base * (blocks + 2) + order[None, None, :])
    li = pick(base * left_count + notes[:, :1])
    slot_rows = pick(notes[:, 1:])
    local_right = line[:, None, :] - my_z * (q * right_count)
    ri = pick(local_right)
    my_dims = lax.dynamic_slice_in_dim(right_dims, my_z * (q * right_count), q * right_count)
    slot_cols = jnp.sum(
        jnp.where(ri[:, None] == jnp.arange(q * right_count, dtype=jnp.int32)[None, :],
                  my_dims[None, :], 0), axis=1)
    out, stat = apply_blocks(li, ri, pi, ok, slot_rows, slot_cols, psi_all, left_all, right_all)
    ph, pp = jnp.sum(stat[:, 0]), jnp.sum(stat[:, 1])
    local = jnp.where(pp > 0, ph / jnp.where(pp > 0, pp, 1.0), 0.0)
    ss = jnp.sum(stat[:, 2] + (stat[:, 3] - local) ** 2 * stat[:, 1])
    stat = jnp.broadcast_to(jnp.pad(jnp.stack([ph, pp, ss, local]), (0, 4))[:, None], (8, 128))
    back, stat_all = give_back(p, q, out.reshape(p, slots // 2, tile, 2 * tile), stat)

    own_rank = lax.dynamic_index_in_dim(rank, my_z, 0, keepdims=False)
    target = (own_sector // (right_count * q)) * slots + own_rank
    got = jnp.take(back.reshape(p * slots // 2, tile, 2 * tile), target // 2, axis=0)
    got = jnp.where((target % 2 == 0)[:, None, None], got[:, :, :tile], got[:, :, tile:])
    hpsi = jnp.where(mask, got, jnp.float32(0.0))

    psi_float = psi_used.astype(jnp.float32)
    stat_all = stat_all[:, :4, 0]
    theta = jnp.sum(stat_all[:, 0]) / jnp.sum(stat_all[:, 1])
    gap = stat_all[:, 3] - theta
    spread = jnp.sum(stat_all[:, 2] + gap * gap * stat_all[:, 1])
    resid = hpsi - theta * psi_float
    scale = jnp.sqrt(spread / (blocks * owners * tile * tile) + 1e-06)
    return (hpsi, resid / scale, jnp.reshape(theta, (1,)))


def solution(mesh):
    placed = (
        P(("groups", "sector"), None, None),
        P(("groups", "sector")),
        P(("groups", "sector")),
        P("groups"),
        P("groups"),
        P(("groups", "sector"), None, None),
        P(("groups", "sector"), None, None),
    )
    return jax.shard_map(
        body,
        mesh=mesh,
        in_specs=placed,
        out_specs=(
            P(("groups", "sector"), None, None),
            P(("groups", "sector"), None, None),
            P("groups"),
        ),
        check_vma=False,
    )
```

```python
import functools

import jax
import jax.numpy as jnp
from jax import lax
from jax.experimental import pallas as pl
from jax.experimental.pallas import tpu as pltpu
from jax.sharding import PartitionSpec as P


def peer(index):
    return dict(device_id={"sector": index}, device_id_type=pl.DeviceIdType.MESH)


def gather_kernel(p, q, chunks, left, right, psi, left_all, right_all, psi_all,
                  l_send, l_recv, s_send, s_recv, r_send, r_recv, own_sem):
    device = lax.axis_index("sector")
    z, y = device // q, device % q
    mate = z * q + (y // 2) * 2 + (1 - y % 2)
    across = z * q + (y + 2) % q
    across_y = (y + 2) % q
    n = left.shape[0] // chunks
    rights = right.shape[0]
    has_up, has_down = z + 1 < p, z > 0

    barrier = pltpu.get_barrier_semaphore()
    pl.semaphore_signal(barrier, inc=1, **peer(mate))
    pl.semaphore_signal(barrier, inc=1, **peer(across))

    @pl.when(has_up)
    def _():
        pl.semaphore_signal(barrier, inc=1, **peer(device + q))

    @pl.when(has_down)
    def _():
        pl.semaphore_signal(barrier, inc=1, **peer(device - q))

    pl.semaphore_wait(barrier, 4 - (z + 1) // p - (p - z) // p)

    own = [
        pltpu.make_async_copy(left, left_all.at[z], own_sem.at[0]),
        pltpu.make_async_copy(right, right_all.at[y], own_sem.at[1]),
        pltpu.make_async_copy(psi, psi_all.at[z], own_sem.at[2]),
    ]

    def l_copy(way, t, c, shard):
        part = pl.ds(c * n, n)
        src = left.at[part] if t == 0 else left_all.at[shard, part]
        return pltpu.make_async_remote_copy(
            src, left_all.at[shard, part], l_send.at[way, t, c], l_recv.at[way, t, c],
            **peer(device + (q if way == 0 else -q)))

    def s_copy(way, t, shard):
        src = psi if t == 0 else psi_all.at[shard]
        return pltpu.make_async_remote_copy(
            src, psi_all.at[shard], s_send.at[way, t], s_recv.at[way, t],
            **peer(device + (q if way == 0 else -q)))

    def out_shard(way, t):
        return z - t if way == 0 else z + t

    def sends(way, t):
        return ((z - t >= 0) & has_up) if way == 0 else ((z + t < p) & has_down)

    def in_shard(way, t):
        return z - 1 - t if way == 0 else z + 1 + t

    def gets(way, t):
        return (z - 1 - t >= 0) if way == 0 else (z + 1 + t < p)

    def r_copy(kind, c):
        if kind == 0:
            src, dst, to = right.at[c], right_all.at[y, c], across
        elif kind == 1:
            src, dst, to = right.at[c], right_all.at[y, c], mate
        else:
            src, dst, to = right_all.at[across_y, c], right_all.at[across_y, c], mate
        return pltpu.make_async_remote_copy(
            src, dst, r_send.at[kind, c], r_recv.at[kind, c], **peer(to))

    def r_forward(c):
        r_copy(0, c).wait_recv()
        r_copy(2, c).start()

    merged = p > 3 and 2 * chunks == rights

    for t in range(p):
        if t < p - 1:
            for way in (0, 1):
                if t > 0:
                    @pl.when(gets(way, t - 1))
                    def _(way=way, t=t):
                        s_copy(way, t - 1, in_shard(way, t - 1)).wait_recv()

                @pl.when(sends(way, t))
                def _(way=way, t=t):
                    s_copy(way, t, out_shard(way, t)).start()

        def step(c, carry, t=t):
            for way in (0, 1):
                if t > 0:
                    @pl.when(gets(way, t - 1))
                    def _(way=way):
                        l_copy(way, t - 1, c, in_shard(way, t - 1)).wait_recv()

                if t < p - 1:
                    @pl.when(sends(way, t))
                    def _(way=way):
                        l_copy(way, t, c, out_shard(way, t)).start()
            if merged and t < 2:
                r_copy(0, t * chunks + c).start()
                r_copy(1, t * chunks + c).start()
            if merged and t in (1, 2):
                r_forward((t - 1) * chunks + c)
            return carry

        lax.fori_loop(0, chunks, step, 0)
        if t == 0:
            if not merged:
                def first(c, carry):
                    r_copy(0, c).start()
                    r_copy(1, c).start()
                    return carry

                lax.fori_loop(0, rights, first, 0)
            for copy in own:
                copy.start()

    for way in (0, 1):
        @pl.when(gets(way, p - 2))
        def _(way=way):
            s_copy(way, p - 2, in_shard(way, p - 2)).wait_recv()

    if not merged:
        def rest(c, carry):
            r_forward(c)
            return carry

        lax.fori_loop(0, rights, rest, 0)

    def finish(c, carry):
        r_copy(0, c).wait_send()
        r_copy(1, c).wait_send()
        r_copy(2, c).wait_send()
        r_copy(1, c).wait_recv()
        r_copy(2, c).wait_recv()
        return carry

    lax.fori_loop(0, rights, finish, 0)
    for t in range(p - 1):
        for way in (0, 1):
            @pl.when(sends(way, t))
            def _(way=way, t=t):
                s_copy(way, t, out_shard(way, t)).wait_send()

                def drain(c, carry):
                    l_copy(way, t, c, out_shard(way, t)).wait_send()
                    return carry

                lax.fori_loop(0, chunks, drain, 0)
    for copy in own:
        copy.wait()


def gather(p, q, left, right, psi):
    chunks = left.shape[0] if p <= 4 else 2
    anyspace = pl.BlockSpec(memory_space=pl.ANY)
    dma = pltpu.SemaphoreType.DMA
    return pl.pallas_call(
        functools.partial(gather_kernel, p, q, chunks),
        out_shape=(
            jax.ShapeDtypeStruct((p,) + left.shape, left.dtype),
            jax.ShapeDtypeStruct((q,) + right.shape, right.dtype),
            jax.ShapeDtypeStruct((p,) + psi.shape, psi.dtype),
        ),
        in_specs=[anyspace] * 3,
        out_specs=(anyspace,) * 3,
        scratch_shapes=[
            dma((2, p - 1, chunks)), dma((2, p - 1, chunks)),
            dma((2, p - 1)), dma((2, p - 1)),
            dma((3, right.shape[0])), dma((3, right.shape[0])), dma((3,)),
        ],
        compiler_params=pltpu.CompilerParams(collective_id=0, has_side_effects=True),
    )(left, right, psi)


def return_kernel(p, q, out, stat, back, stat_all, send, recv, st_send, st_recv, own_sem):
    device = lax.axis_index("sector")
    owners = p * q
    z, y = device // q, device % q
    barrier = pltpu.get_barrier_semaphore()

    def greet(d, carry):
        pl.semaphore_signal(barrier, inc=1, **peer((device + d) % owners))
        return carry

    lax.fori_loop(1, owners, greet, 0)
    pl.semaphore_wait(barrier, owners - 1)

    def tiles(d):
        to = (z + d) % p
        return pltpu.make_async_remote_copy(
            out.at[to], back.at[z], send.at[d], recv.at[d], **peer(to * q + y))

    def stats(d):
        return pltpu.make_async_remote_copy(
            stat, stat_all.at[device], st_send.at[d], st_recv.at[d],
            **peer((device + d) % owners))

    def each(low, high, act):
        def step(d, carry):
            act(d)
            return carry

        lax.fori_loop(low, high, step, 0)

    own = [
        pltpu.make_async_copy(out.at[z], back.at[z], own_sem.at[0]),
        pltpu.make_async_copy(stat, stat_all.at[device], own_sem.at[1]),
    ]
    each(1, owners, lambda d: stats(d).start())
    each(1, p, lambda d: tiles(d).start())
    for copy in own:
        copy.start()
    each(1, owners, lambda d: stats(d).wait())
    each(1, p, lambda d: tiles(d).wait())
    for copy in own:
        copy.wait()


def give_back(p, q, out, stat):
    anyspace = pl.BlockSpec(memory_space=pl.ANY)
    dma = pltpu.SemaphoreType.DMA
    return pl.pallas_call(
        functools.partial(return_kernel, p, q),
        out_shape=(
            jax.ShapeDtypeStruct(out.shape, out.dtype),
            jax.ShapeDtypeStruct((p * q,) + stat.shape, stat.dtype),
        ),
        in_specs=[anyspace] * 2,
        out_specs=(anyspace,) * 2,
        scratch_shapes=[dma((p,)), dma((p,)), dma((p * q,)), dma((p * q,)), dma((2,))],
        compiler_params=pltpu.CompilerParams(collective_id=1, has_side_effects=True),
    )(out, stat)


def apply_kernel(li, ri, pi, ok, rows, cols, psi0, psi1, l0, l1, r0, r1, out_ref, stat_ref):
    s = pl.program_id(0) * 2
    tile = l0.shape[1]
    wide = 4 * tile
    chunks = l0.shape[2] // wide
    live = ok[s] + ok[s + 1]

    @pl.when(live > 0)
    def _():
        ia = lax.broadcasted_iota(jnp.int32, (wide, wide), 0) // tile
        ib = lax.broadcasted_iota(jnp.int32, (wide, wide), 1) // tile
        a = lax.broadcasted_iota(jnp.int32, (tile, tile), 0)
        e = lax.broadcasted_iota(jnp.int32, (tile, tile), 1)
        psis, diags = [], []
        for half, psi_ref in enumerate((psi0, psi1)):
            pair = psi_ref[0].astype(jnp.float32)
            psi_f = jnp.where(pi[s + half] % 2 == 0, pair[:, :tile], pair[:, tile:])
            psi_f = jnp.where(ok[s + half] > 0, psi_f, 0.0)
            psi = psi_f.astype(jnp.bfloat16)
            row = jnp.concatenate([psi] * 4, axis=1)
            full = jnp.concatenate([row] * 4, axis=0)
            psis.append(psi_f)
            diags.append(jnp.where(ia == ib, full, jnp.zeros_like(full)))
        parts = [[], []]
        for k in range(chunks):
            cut = slice(k * wide, (k + 1) * wide)
            for half, l_ref in enumerate((l0, l1)):
                t = jnp.dot(l_ref[0, :, cut], diags[half], preferred_element_type=jnp.float32)
                parts[half].append(t.astype(jnp.bfloat16))
        for half, r_ref in enumerate((r0, r1)):
            lanes = slice(half * tile, (half + 1) * tile)
            t = jnp.concatenate(parts[half], axis=1)
            acc = lax.dot_general(t, r_ref[0], (((1,), (1,)), ((), ())),
                                  preferred_element_type=jnp.float32)
            acc = jnp.where((a < rows[s + half]) & (e < cols[s + half]) & (ok[s + half] > 0), acc, 0.0)
            psi_f = psis[half]
            out_ref[0, :, lanes] = acc
            ph = jnp.sum(psi_f * acc, axis=0, keepdims=True)
            pp = jnp.sum(psi_f * psi_f, axis=0, keepdims=True)
            th = jnp.where(pp > 0, ph / jnp.where(pp > 0, pp, 1.0), 0.0)
            rest = acc - th * psi_f
            stat_ref[0, 0:1, lanes] = ph
            stat_ref[0, 1:2, lanes] = pp
            stat_ref[0, 2:3, lanes] = jnp.sum(rest * rest, axis=0, keepdims=True)
            stat_ref[0, 3:4, lanes] = th

    @pl.when(live == 0)
    def _():
        out_ref[...] = jnp.zeros_like(out_ref)
        stat_ref[...] = jnp.zeros_like(stat_ref)


def apply_blocks(li, ri, pi, ok, rows, cols, psi, left, right):
    pairs = li.shape[0] // 2
    tile = left.shape[1]
    width = left.shape[2]

    def spec(shape, which, half, scale=1):
        return pl.BlockSpec((1,) + shape, lambda j, *ids: (ids[which][2 * j + half] // scale, 0, 0))

    return pl.pallas_call(
        apply_kernel,
        grid_spec=pltpu.PrefetchScalarGridSpec(
            num_scalar_prefetch=6,
            grid=(pairs,),
            in_specs=[
                spec((tile, 2 * tile), 2, 0, 2), spec((tile, 2 * tile), 2, 1, 2),
                spec((tile, width), 0, 0), spec((tile, width), 0, 1),
                spec((tile, width), 1, 0), spec((tile, width), 1, 1),
            ],
            out_specs=[
                pl.BlockSpec((1, tile, 2 * tile), lambda j, *ids: (j, 0, 0)),
                pl.BlockSpec((1, 4, 2 * tile), lambda j, *ids: (j, 0, 0)),
            ],
        ),
        out_shape=[
            jax.ShapeDtypeStruct((pairs, tile, 2 * tile), jnp.float32),
            jax.ShapeDtypeStruct((pairs, 4, 2 * tile), jnp.float32),
        ],
        compiler_params=pltpu.CompilerParams(vmem_limit_bytes=56 * 1024 * 1024),
    )(li, ri, pi, ok, rows, cols, psi, psi, left, left, right, right)


def body(psi_blocks, left_sector, left_dims, right_sector, right_dims, left_env, right_env):
    blocks, tile = psi_blocks.shape[:2]
    left_count = left_env.shape[0]
    right_count = right_env.shape[0]
    owners = lax.axis_size("sector")
    device = lax.axis_index("sector")
    cap = (2 * blocks + owners - 1) // owners
    q = 4
    p = owners // q
    slots = min(q * cap, blocks)
    my_z, my_y = device // q, device % q

    left_local = left_sector - device * left_count
    table = right_sector.reshape(owners, blocks)
    own_sector = lax.dynamic_index_in_dim(table, device, 0, keepdims=False)
    rows = jnp.sum(
        jnp.where(left_local[:, None] == jnp.arange(left_count, dtype=jnp.int32)[None, :],
                  left_dims[None, :], 0), axis=1)
    cols = jnp.sum(
        jnp.where(own_sector[:, None] == jnp.arange(right_dims.shape[0], dtype=jnp.int32)[None, :],
                  right_dims[None, :], 0), axis=1)
    place = jnp.arange(tile, dtype=jnp.int32)
    mask = (place[None, :, None] < rows[:, None, None]) & (
        place[None, None, :] < cols[:, None, None])
    psi_used = jnp.where(mask, psi_blocks, jnp.zeros_like(psi_blocks))
    half = blocks // 2
    packed = psi_used.reshape(half, 2, tile, tile).transpose(0, 2, 1, 3).reshape(half, tile, 2 * tile)
    extra = jnp.pad(jnp.stack([left_local, rows]).astype(jnp.bfloat16),
                    ((0, tile - 2), (0, 2 * tile - blocks)))
    sent = jnp.concatenate([packed, extra[None]], axis=0)

    left_all, right_all, psi_all = gather(p, q, left_env, right_env, sent)
    notes = psi_all[:, half, :2, :blocks].astype(jnp.int32)
    left_all = left_all.reshape(p * left_count, tile, -1)
    right_all = right_all.reshape(q * right_count, tile, -1)
    psi_all = psi_all.reshape(p * (half + 1), tile, 2 * tile)

    line = lax.dynamic_index_in_dim(table.reshape(p, q, blocks), my_y, 1, keepdims=False)
    goal = line // (right_count * q)
    order = jnp.arange(blocks, dtype=jnp.int32)
    same = (goal[:, :, None] == goal[:, None, :]) & (order[None, None, :] < order[None, :, None])
    rank = jnp.sum(same.astype(jnp.int32), axis=2)
    match = (goal[:, None, :] == my_z) & (
        rank[:, None, :] == jnp.arange(slots, dtype=jnp.int32)[None, :, None])

    def pick(values):
        return jnp.sum(jnp.where(match, values, 0), axis=2).reshape(p * slots)

    ok = pick(jnp.ones((p, 1, blocks), jnp.int32))
    base = jnp.arange(p, dtype=jnp.int32)[:, None, None]
    pi = pick(base * (blocks + 2) + order[None, None, :])
    li = pick(base * left_count + notes[:, :1])
    slot_rows = pick(notes[:, 1:])
    local_right = line[:, None, :] - my_z * (q * right_count)
    ri = pick(local_right)
    my_dims = lax.dynamic_slice_in_dim(right_dims, my_z * (q * right_count), q * right_count)
    slot_cols = jnp.sum(
        jnp.where(ri[:, None] == jnp.arange(q * right_count, dtype=jnp.int32)[None, :],
                  my_dims[None, :], 0), axis=1)
    out, stat = apply_blocks(li, ri, pi, ok, slot_rows, slot_cols, psi_all, left_all, right_all)
    ph, pp = jnp.sum(stat[:, 0]), jnp.sum(stat[:, 1])
    local = jnp.where(pp > 0, ph / jnp.where(pp > 0, pp, 1.0), 0.0)
    ss = jnp.sum(stat[:, 2] + (stat[:, 3] - local) ** 2 * stat[:, 1])
    stat = jnp.broadcast_to(jnp.pad(jnp.stack([ph, pp, ss, local]), (0, 4))[:, None], (8, 128))
    back, stat_all = give_back(p, q, out.reshape(p, slots // 2, tile, 2 * tile), stat)

    own_rank = lax.dynamic_index_in_dim(rank, my_z, 0, keepdims=False)
    target = (own_sector // (right_count * q)) * slots + own_rank
    got = jnp.take(back.reshape(p * slots // 2, tile, 2 * tile), target // 2, axis=0)
    got = jnp.where((target % 2 == 0)[:, None, None], got[:, :, :tile], got[:, :, tile:])
    hpsi = jnp.where(mask, got, jnp.float32(0.0))

    psi_float = psi_used.astype(jnp.float32)
    stat_all = stat_all[:, :4, 0]
    theta = jnp.sum(stat_all[:, 0]) / jnp.sum(stat_all[:, 1])
    gap = stat_all[:, 3] - theta
    spread = jnp.sum(stat_all[:, 2] + gap * gap * stat_all[:, 1])
    resid = hpsi - theta * psi_float
    scale = jnp.sqrt(spread / (blocks * owners * tile * tile) + 1e-06)
    return (hpsi, resid / scale, jnp.reshape(theta, (1,)))


def solution(mesh):
    placed = (
        P(("groups", "sector"), None, None),
        P(("groups", "sector")),
        P(("groups", "sector")),
        P("groups"),
        P("groups"),
        P(("groups", "sector"), None, None),
        P(("groups", "sector"), None, None),
    )
    return jax.shard_map(
        body,
        mesh=mesh,
        in_specs=placed,
        out_specs=(
            P(("groups", "sector"), None, None),
            P(("groups", "sector"), None, None),
            P("groups"),
        ),
        check_vma=False,
    )
```

```python
import functools

import jax
import jax.numpy as jnp
from jax import lax
from jax.experimental import pallas as pl
from jax.experimental.pallas import tpu as pltpu
from jax.sharding import PartitionSpec as P


def peer(index):
    return dict(device_id={"sector": index}, device_id_type=pl.DeviceIdType.MESH)


def gather_kernel(p, q, chunks, left, right, psi, left_all, right_all, psi_all,
                  l_send, l_recv, s_send, s_recv, r_send, r_recv, own_sem):
    device = lax.axis_index("sector")
    z, y = device // q, device % q
    mate = z * q + (y // 2) * 2 + (1 - y % 2)
    across = z * q + (y + 2) % q
    across_y = (y + 2) % q
    n = left.shape[0] // chunks
    rights = right.shape[0]
    has_up, has_down = z + 1 < p, z > 0

    barrier = pltpu.get_barrier_semaphore()
    pl.semaphore_signal(barrier, inc=1, **peer(mate))
    pl.semaphore_signal(barrier, inc=1, **peer(across))

    @pl.when(has_up)
    def _():
        pl.semaphore_signal(barrier, inc=1, **peer(device + q))

    @pl.when(has_down)
    def _():
        pl.semaphore_signal(barrier, inc=1, **peer(device - q))

    pl.semaphore_wait(barrier, 4 - (z + 1) // p - (p - z) // p)

    own = [
        pltpu.make_async_copy(left, left_all.at[z], own_sem.at[0]),
        pltpu.make_async_copy(right, right_all.at[y], own_sem.at[1]),
        pltpu.make_async_copy(psi, psi_all.at[z], own_sem.at[2]),
    ]

    def l_copy(way, t, c, shard):
        part = pl.ds(c * n, n)
        src = left.at[part] if t == 0 else left_all.at[shard, part]
        return pltpu.make_async_remote_copy(
            src, left_all.at[shard, part], l_send.at[way, t, c], l_recv.at[way, t, c],
            **peer(device + (q if way == 0 else -q)))

    def s_copy(way, t, shard):
        src = psi if t == 0 else psi_all.at[shard]
        return pltpu.make_async_remote_copy(
            src, psi_all.at[shard], s_send.at[way, t], s_recv.at[way, t],
            **peer(device + (q if way == 0 else -q)))

    def out_shard(way, t):
        return z - t if way == 0 else z + t

    def sends(way, t):
        return ((z - t >= 0) & has_up) if way == 0 else ((z + t < p) & has_down)

    def in_shard(way, t):
        return z - 1 - t if way == 0 else z + 1 + t

    def gets(way, t):
        return (z - 1 - t >= 0) if way == 0 else (z + 1 + t < p)

    def r_copy(kind, c):
        if kind == 0:
            src, dst, to = right.at[c], right_all.at[y, c], across
        elif kind == 1:
            src, dst, to = right.at[c], right_all.at[y, c], mate
        else:
            src, dst, to = right_all.at[across_y, c], right_all.at[across_y, c], mate
        return pltpu.make_async_remote_copy(
            src, dst, r_send.at[kind, c], r_recv.at[kind, c], **peer(to))

    def r_forward(c):
        r_copy(0, c).wait_recv()
        r_copy(2, c).start()

    merged = p > 3 and 2 * chunks == rights

    for t in range(p):
        if t < p - 1:
            for way in (0, 1):
                if t > 0:
                    @pl.when(gets(way, t - 1))
                    def _(way=way, t=t):
                        s_copy(way, t - 1, in_shard(way, t - 1)).wait_recv()

                @pl.when(sends(way, t))
                def _(way=way, t=t):
                    s_copy(way, t, out_shard(way, t)).start()

        def step(c, carry, t=t):
            for way in (0, 1):
                if t > 0:
                    @pl.when(gets(way, t - 1))
                    def _(way=way):
                        l_copy(way, t - 1, c, in_shard(way, t - 1)).wait_recv()

                if t < p - 1:
                    @pl.when(sends(way, t))
                    def _(way=way):
                        l_copy(way, t, c, out_shard(way, t)).start()
            if merged and t < 2:
                r_copy(0, t * chunks + c).start()
                r_copy(1, t * chunks + c).start()
            if merged and t in (1, 2):
                r_forward((t - 1) * chunks + c)
            return carry

        lax.fori_loop(0, chunks, step, 0)
        if t == 0:
            if not merged:
                def first(c, carry):
                    r_copy(0, c).start()
                    r_copy(1, c).start()
                    return carry

                lax.fori_loop(0, rights, first, 0)
            for copy in own:
                copy.start()

    for way in (0, 1):
        @pl.when(gets(way, p - 2))
        def _(way=way):
            s_copy(way, p - 2, in_shard(way, p - 2)).wait_recv()

    if not merged:
        def rest(c, carry):
            r_forward(c)
            return carry

        lax.fori_loop(0, rights, rest, 0)

    def finish(c, carry):
        r_copy(0, c).wait_send()
        r_copy(1, c).wait_send()
        r_copy(2, c).wait_send()
        r_copy(1, c).wait_recv()
        r_copy(2, c).wait_recv()
        return carry

    lax.fori_loop(0, rights, finish, 0)
    for t in range(p - 1):
        for way in (0, 1):
            @pl.when(sends(way, t))
            def _(way=way, t=t):
                s_copy(way, t, out_shard(way, t)).wait_send()

                def drain(c, carry):
                    l_copy(way, t, c, out_shard(way, t)).wait_send()
                    return carry

                lax.fori_loop(0, chunks, drain, 0)
    for copy in own:
        copy.wait()


def gather(p, q, left, right, psi):
    chunks = left.shape[0] if p <= 4 else 2
    anyspace = pl.BlockSpec(memory_space=pl.ANY)
    dma = pltpu.SemaphoreType.DMA
    return pl.pallas_call(
        functools.partial(gather_kernel, p, q, chunks),
        out_shape=(
            jax.ShapeDtypeStruct((p,) + left.shape, left.dtype),
            jax.ShapeDtypeStruct((q,) + right.shape, right.dtype),
            jax.ShapeDtypeStruct((p,) + psi.shape, psi.dtype),
        ),
        in_specs=[anyspace] * 3,
        out_specs=(anyspace,) * 3,
        scratch_shapes=[
            dma((2, p - 1, chunks)), dma((2, p - 1, chunks)),
            dma((2, p - 1)), dma((2, p - 1)),
            dma((3, right.shape[0])), dma((3, right.shape[0])), dma((3,)),
        ],
        compiler_params=pltpu.CompilerParams(collective_id=0, has_side_effects=True),
    )(left, right, psi)


def return_kernel(p, q, out, stat, back, stat_all, send, recv, st_send, st_recv, own_sem):
    device = lax.axis_index("sector")
    owners = p * q
    z, y = device // q, device % q
    barrier = pltpu.get_barrier_semaphore()

    def greet(d, carry):
        pl.semaphore_signal(barrier, inc=1, **peer((device + d) % owners))
        return carry

    lax.fori_loop(1, owners, greet, 0)
    pl.semaphore_wait(barrier, owners - 1)

    def tiles(d):
        to = (z + d) % p
        return pltpu.make_async_remote_copy(
            out.at[to], back.at[z], send.at[d], recv.at[d], **peer(to * q + y))

    def stats(d):
        return pltpu.make_async_remote_copy(
            stat, stat_all.at[device], st_send.at[d], st_recv.at[d],
            **peer((device + d) % owners))

    def each(low, high, act):
        def step(d, carry):
            act(d)
            return carry

        lax.fori_loop(low, high, step, 0)

    own = [
        pltpu.make_async_copy(out.at[z], back.at[z], own_sem.at[0]),
        pltpu.make_async_copy(stat, stat_all.at[device], own_sem.at[1]),
    ]
    each(1, owners, lambda d: stats(d).start())
    each(1, p, lambda d: tiles(d).start())
    for copy in own:
        copy.start()
    each(1, owners, lambda d: stats(d).wait())
    each(1, p, lambda d: tiles(d).wait())
    for copy in own:
        copy.wait()


def give_back(p, q, out, stat):
    anyspace = pl.BlockSpec(memory_space=pl.ANY)
    dma = pltpu.SemaphoreType.DMA
    return pl.pallas_call(
        functools.partial(return_kernel, p, q),
        out_shape=(
            jax.ShapeDtypeStruct(out.shape, out.dtype),
            jax.ShapeDtypeStruct((p * q,) + stat.shape, stat.dtype),
        ),
        in_specs=[anyspace] * 2,
        out_specs=(anyspace,) * 2,
        scratch_shapes=[dma((p,)), dma((p,)), dma((p * q,)), dma((p * q,)), dma((2,))],
        compiler_params=pltpu.CompilerParams(collective_id=1, has_side_effects=True),
    )(out, stat)


def apply_kernel(li, ri, pi, ok, rows, cols, psi0, psi1, l0, l1, r0, r1, out_ref, stat_ref):
    s = pl.program_id(0) * 2
    tile = l0.shape[1]
    wide = 4 * tile
    chunks = l0.shape[2] // wide
    live = ok[s] + ok[s + 1]

    @pl.when(live > 0)
    def _():
        ia = lax.broadcasted_iota(jnp.int32, (wide, wide), 0) // tile
        ib = lax.broadcasted_iota(jnp.int32, (wide, wide), 1) // tile
        a = lax.broadcasted_iota(jnp.int32, (tile, tile), 0)
        e = lax.broadcasted_iota(jnp.int32, (tile, tile), 1)
        psis, diags = [], []
        for half, psi_ref in enumerate((psi0, psi1)):
            pair = psi_ref[0].astype(jnp.float32)
            psi_f = jnp.where(pi[s + half] % 2 == 0, pair[:, :tile], pair[:, tile:])
            psi_f = jnp.where(ok[s + half] > 0, psi_f, 0.0)
            psi = psi_f.astype(jnp.bfloat16)
            row = jnp.concatenate([psi] * 4, axis=1)
            full = jnp.concatenate([row] * 4, axis=0)
            psis.append(psi_f)
            diags.append(jnp.where(ia == ib, full, jnp.zeros_like(full)))
        parts = [[], []]
        for k in range(chunks):
            cut = slice(k * wide, (k + 1) * wide)
            for half, l_ref in enumerate((l0, l1)):
                t = jnp.dot(l_ref[0, :, cut], diags[half], preferred_element_type=jnp.float32)
                parts[half].append(t.astype(jnp.bfloat16))
        for half, r_ref in enumerate((r0, r1)):
            lanes = slice(half * tile, (half + 1) * tile)
            t = jnp.concatenate(parts[half], axis=1)
            acc = lax.dot_general(t, r_ref[0], (((1,), (1,)), ((), ())),
                                  preferred_element_type=jnp.float32)
            acc = jnp.where((a < rows[s + half]) & (e < cols[s + half]) & (ok[s + half] > 0), acc, 0.0)
            psi_f = psis[half]
            out_ref[0, :, lanes] = acc
            ph = jnp.sum(psi_f * acc, axis=0, keepdims=True)
            pp = jnp.sum(psi_f * psi_f, axis=0, keepdims=True)
            th = jnp.where(pp > 0, ph / jnp.where(pp > 0, pp, 1.0), 0.0)
            rest = acc - th * psi_f
            stat_ref[0, 0:1, lanes] = ph
            stat_ref[0, 1:2, lanes] = pp
            stat_ref[0, 2:3, lanes] = jnp.sum(rest * rest, axis=0, keepdims=True)
            stat_ref[0, 3:4, lanes] = th

    @pl.when(live == 0)
    def _():
        out_ref[...] = jnp.zeros_like(out_ref)
        stat_ref[...] = jnp.zeros_like(stat_ref)


def apply_blocks(li, ri, pi, ok, rows, cols, psi, left, right):
    pairs = li.shape[0] // 2
    tile = left.shape[1]
    width = left.shape[2]

    def spec(shape, which, half, scale=1):
        return pl.BlockSpec((1,) + shape, lambda j, *ids: (ids[which][2 * j + half] // scale, 0, 0))

    return pl.pallas_call(
        apply_kernel,
        grid_spec=pltpu.PrefetchScalarGridSpec(
            num_scalar_prefetch=6,
            grid=(pairs,),
            in_specs=[
                spec((tile, 2 * tile), 2, 0, 2), spec((tile, 2 * tile), 2, 1, 2),
                spec((tile, width), 0, 0), spec((tile, width), 0, 1),
                spec((tile, width), 1, 0), spec((tile, width), 1, 1),
            ],
            out_specs=[
                pl.BlockSpec((1, tile, 2 * tile), lambda j, *ids: (j, 0, 0)),
                pl.BlockSpec((1, 4, 2 * tile), lambda j, *ids: (j, 0, 0)),
            ],
        ),
        out_shape=[
            jax.ShapeDtypeStruct((pairs, tile, 2 * tile), jnp.float32),
            jax.ShapeDtypeStruct((pairs, 4, 2 * tile), jnp.float32),
        ],
        compiler_params=pltpu.CompilerParams(vmem_limit_bytes=56 * 1024 * 1024),
    )(li, ri, pi, ok, rows, cols, psi, psi, left, left, right, right)


def body(psi_blocks, left_sector, left_dims, right_sector, right_dims, left_env, right_env):
    blocks, tile = psi_blocks.shape[:2]
    left_count = left_env.shape[0]
    right_count = right_env.shape[0]
    owners = lax.axis_size("sector")
    device = lax.axis_index("sector")
    cap = (2 * blocks + owners - 1) // owners
    q = 4
    p = owners // q
    slots = min(q * cap, blocks)
    my_z, my_y = device // q, device % q

    left_local = left_sector - device * left_count
    table = right_sector.reshape(owners, blocks)
    own_sector = lax.dynamic_index_in_dim(table, device, 0, keepdims=False)
    rows = jnp.sum(
        jnp.where(left_local[:, None] == jnp.arange(left_count, dtype=jnp.int32)[None, :],
                  left_dims[None, :], 0), axis=1)
    cols = jnp.sum(
        jnp.where(own_sector[:, None] == jnp.arange(right_dims.shape[0], dtype=jnp.int32)[None, :],
                  right_dims[None, :], 0), axis=1)
    place = jnp.arange(tile, dtype=jnp.int32)
    mask = (place[None, :, None] < rows[:, None, None]) & (
        place[None, None, :] < cols[:, None, None])
    psi_used = jnp.where(mask, psi_blocks, jnp.zeros_like(psi_blocks))
    half = blocks // 2
    packed = psi_used.reshape(half, 2, tile, tile).transpose(0, 2, 1, 3).reshape(half, tile, 2 * tile)
    extra = jnp.pad(jnp.stack([left_local, rows]).astype(jnp.bfloat16),
                    ((0, tile - 2), (0, 2 * tile - blocks)))
    sent = jnp.concatenate([packed, extra[None]], axis=0)

    left_all, right_all, psi_all = gather(
        p, q, left_env.reshape(2 * left_count, tile // 2, -1),
        right_env.reshape(2 * right_count, tile // 2, -1), sent)
    notes = psi_all[:, half, :2, :blocks].astype(jnp.int32)
    left_all = left_all.reshape(p * left_count, tile, -1)
    right_all = right_all.reshape(q * right_count, tile, -1)
    psi_all = psi_all.reshape(p * (half + 1), tile, 2 * tile)

    line = lax.dynamic_index_in_dim(table.reshape(p, q, blocks), my_y, 1, keepdims=False)
    goal = line // (right_count * q)
    order = jnp.arange(blocks, dtype=jnp.int32)
    same = (goal[:, :, None] == goal[:, None, :]) & (order[None, None, :] < order[None, :, None])
    rank = jnp.sum(same.astype(jnp.int32), axis=2)
    match = (goal[:, None, :] == my_z) & (
        rank[:, None, :] == jnp.arange(slots, dtype=jnp.int32)[None, :, None])

    def pick(values):
        return jnp.sum(jnp.where(match, values, 0), axis=2).reshape(p * slots)

    ok = pick(jnp.ones((p, 1, blocks), jnp.int32))
    base = jnp.arange(p, dtype=jnp.int32)[:, None, None]
    pi = pick(base * (blocks + 2) + order[None, None, :])
    li = pick(base * left_count + notes[:, :1])
    slot_rows = pick(notes[:, 1:])
    local_right = line[:, None, :] - my_z * (q * right_count)
    ri = pick(local_right)
    my_dims = lax.dynamic_slice_in_dim(right_dims, my_z * (q * right_count), q * right_count)
    slot_cols = jnp.sum(
        jnp.where(ri[:, None] == jnp.arange(q * right_count, dtype=jnp.int32)[None, :],
                  my_dims[None, :], 0), axis=1)
    out, stat = apply_blocks(li, ri, pi, ok, slot_rows, slot_cols, psi_all, left_all, right_all)
    ph, pp = jnp.sum(stat[:, 0]), jnp.sum(stat[:, 1])
    local = jnp.where(pp > 0, ph / jnp.where(pp > 0, pp, 1.0), 0.0)
    ss = jnp.sum(stat[:, 2] + (stat[:, 3] - local) ** 2 * stat[:, 1])
    stat = jnp.broadcast_to(jnp.pad(jnp.stack([ph, pp, ss, local]), (0, 4))[:, None], (8, 128))
    back, stat_all = give_back(p, q, out.reshape(p, slots // 2, tile, 2 * tile), stat)

    own_rank = lax.dynamic_index_in_dim(rank, my_z, 0, keepdims=False)
    target = (own_sector // (right_count * q)) * slots + own_rank
    got = jnp.take(back.reshape(p * slots // 2, tile, 2 * tile), target // 2, axis=0)
    got = jnp.where((target % 2 == 0)[:, None, None], got[:, :, :tile], got[:, :, tile:])
    hpsi = jnp.where(mask, got, jnp.float32(0.0))

    psi_float = psi_used.astype(jnp.float32)
    stat_all = stat_all[:, :4, 0]
    theta = jnp.sum(stat_all[:, 0]) / jnp.sum(stat_all[:, 1])
    gap = stat_all[:, 3] - theta
    spread = jnp.sum(stat_all[:, 2] + gap * gap * stat_all[:, 1])
    resid = hpsi - theta * psi_float
    scale = jnp.sqrt(spread / (blocks * owners * tile * tile) + 1e-06)
    return (hpsi, resid / scale, jnp.reshape(theta, (1,)))


def solution(mesh):
    placed = (
        P(("groups", "sector"), None, None),
        P(("groups", "sector")),
        P(("groups", "sector")),
        P("groups"),
        P("groups"),
        P(("groups", "sector"), None, None),
        P(("groups", "sector"), None, None),
    )
    return jax.shard_map(
        body,
        mesh=mesh,
        in_specs=placed,
        out_specs=(
            P(("groups", "sector"), None, None),
            P(("groups", "sector"), None, None),
            P("groups"),
        ),
        check_vma=False,
    )
```

```python
import functools

import jax
import jax.numpy as jnp
from jax import lax
from jax.experimental import pallas as pl
from jax.experimental.pallas import tpu as pltpu
from jax.sharding import PartitionSpec as P


def peer(index):
    return dict(device_id={"sector": index}, device_id_type=pl.DeviceIdType.MESH)


def gather_kernel(p, q, chunks, left, right, psi, left_all, right_all, psi_all,
                  l_send, l_recv, s_send, s_recv, r_send, r_recv, own_sem):
    device = lax.axis_index("sector")
    z, y = device // q, device % q
    mate = z * q + (y // 2) * 2 + (1 - y % 2)
    across = z * q + (y + 2) % q
    across_y = (y + 2) % q
    n = left.shape[0] // chunks
    rights = right.shape[0]
    has_up, has_down = z + 1 < p, z > 0

    barrier = pltpu.get_barrier_semaphore()
    pl.semaphore_signal(barrier, inc=1, **peer(mate))
    pl.semaphore_signal(barrier, inc=1, **peer(across))

    for d in range(1, p):
        pl.semaphore_signal(barrier, inc=1, **peer(((z + d) % p) * q + y))
    pl.semaphore_wait(barrier, p + 1)

    own = [
        pltpu.make_async_copy(left, left_all.at[z], own_sem.at[0]),
        pltpu.make_async_copy(right, right_all.at[y], own_sem.at[1]),
        pltpu.make_async_copy(psi.at[z], psi_all.at[z], own_sem.at[2]),
    ]

    def l_copy(way, t, c, shard):
        part = pl.ds(c * n, n)
        src = left.at[part] if t == 0 else left_all.at[shard, part]
        return pltpu.make_async_remote_copy(
            src, left_all.at[shard, part], l_send.at[way, t, c], l_recv.at[way, t, c],
            **peer(device + (q if way == 0 else -q)))

    def s_copy(d):
        to = (z + d) % p
        return pltpu.make_async_remote_copy(
            psi.at[to], psi_all.at[z], s_send.at[d], s_recv.at[d], **peer(to * q + y))

    def out_shard(way, t):
        return z - t if way == 0 else z + t

    def sends(way, t):
        return ((z - t >= 0) & has_up) if way == 0 else ((z + t < p) & has_down)

    def in_shard(way, t):
        return z - 1 - t if way == 0 else z + 1 + t

    def gets(way, t):
        return (z - 1 - t >= 0) if way == 0 else (z + 1 + t < p)

    def r_copy(kind, c):
        if kind == 0:
            src, dst, to = right.at[c], right_all.at[y, c], across
        elif kind == 1:
            src, dst, to = right.at[c], right_all.at[y, c], mate
        else:
            src, dst, to = right_all.at[across_y, c], right_all.at[across_y, c], mate
        return pltpu.make_async_remote_copy(
            src, dst, r_send.at[kind, c], r_recv.at[kind, c], **peer(to))

    def r_forward(c):
        r_copy(0, c).wait_recv()
        r_copy(2, c).start()

    merged = p > 3 and 2 * chunks == rights

    for d in range(1, p):
        s_copy(d).start()
    for t in range(p):
        def step(c, carry, t=t):
            for way in (0, 1):
                if t > 0:
                    @pl.when(gets(way, t - 1))
                    def _(way=way):
                        l_copy(way, t - 1, c, in_shard(way, t - 1)).wait_recv()

                if t < p - 1:
                    @pl.when(sends(way, t))
                    def _(way=way):
                        l_copy(way, t, c, out_shard(way, t)).start()
            if merged and t < 2:
                r_copy(0, t * chunks + c).start()
                r_copy(1, t * chunks + c).start()
            if merged and t in (1, 2):
                r_forward((t - 1) * chunks + c)
            return carry

        lax.fori_loop(0, chunks, step, 0)
        if t == 0:
            if not merged:
                def first(c, carry):
                    r_copy(0, c).start()
                    r_copy(1, c).start()
                    return carry

                lax.fori_loop(0, rights, first, 0)
            for copy in own:
                copy.start()

    for d in range(1, p):
        s_copy(d).wait()

    if not merged:
        def rest(c, carry):
            r_forward(c)
            return carry

        lax.fori_loop(0, rights, rest, 0)

    def finish(c, carry):
        r_copy(0, c).wait_send()
        r_copy(1, c).wait_send()
        r_copy(2, c).wait_send()
        r_copy(1, c).wait_recv()
        r_copy(2, c).wait_recv()
        return carry

    lax.fori_loop(0, rights, finish, 0)
    for t in range(p - 1):
        for way in (0, 1):
            @pl.when(sends(way, t))
            def _(way=way, t=t):
                def drain(c, carry):
                    l_copy(way, t, c, out_shard(way, t)).wait_send()
                    return carry

                lax.fori_loop(0, chunks, drain, 0)
    for copy in own:
        copy.wait()


def gather(p, q, left, right, psi):
    chunks = left.shape[0] if p <= 4 else 2
    anyspace = pl.BlockSpec(memory_space=pl.ANY)
    dma = pltpu.SemaphoreType.DMA
    return pl.pallas_call(
        functools.partial(gather_kernel, p, q, chunks),
        out_shape=(
            jax.ShapeDtypeStruct((p,) + left.shape, left.dtype),
            jax.ShapeDtypeStruct((q,) + right.shape, right.dtype),
            jax.ShapeDtypeStruct(psi.shape, psi.dtype),
        ),
        in_specs=[anyspace] * 3,
        out_specs=(anyspace,) * 3,
        scratch_shapes=[
            dma((2, p - 1, chunks)), dma((2, p - 1, chunks)),
            dma((p,)), dma((p,)),
            dma((3, right.shape[0])), dma((3, right.shape[0])), dma((3,)),
        ],
        compiler_params=pltpu.CompilerParams(collective_id=0, has_side_effects=True),
    )(left, right, psi)


def return_kernel(p, q, out, stat, back, stat_all, send, recv, st_send, st_recv, own_sem):
    device = lax.axis_index("sector")
    owners = p * q
    z, y = device // q, device % q
    barrier = pltpu.get_barrier_semaphore()

    def greet(d, carry):
        pl.semaphore_signal(barrier, inc=1, **peer((device + d) % owners))
        return carry

    lax.fori_loop(1, owners, greet, 0)
    pl.semaphore_wait(barrier, owners - 1)

    def tiles(d):
        to = (z + d) % p
        return pltpu.make_async_remote_copy(
            out.at[to], back.at[z], send.at[d], recv.at[d], **peer(to * q + y))

    def stats(d):
        return pltpu.make_async_remote_copy(
            stat, stat_all.at[device], st_send.at[d], st_recv.at[d],
            **peer((device + d) % owners))

    def each(low, high, act):
        def step(d, carry):
            act(d)
            return carry

        lax.fori_loop(low, high, step, 0)

    own = [
        pltpu.make_async_copy(out.at[z], back.at[z], own_sem.at[0]),
        pltpu.make_async_copy(stat, stat_all.at[device], own_sem.at[1]),
    ]
    each(1, owners, lambda d: stats(d).start())
    each(1, p, lambda d: tiles(d).start())
    for copy in own:
        copy.start()
    each(1, owners, lambda d: stats(d).wait())
    each(1, p, lambda d: tiles(d).wait())
    for copy in own:
        copy.wait()


def give_back(p, q, out, stat):
    anyspace = pl.BlockSpec(memory_space=pl.ANY)
    dma = pltpu.SemaphoreType.DMA
    return pl.pallas_call(
        functools.partial(return_kernel, p, q),
        out_shape=(
            jax.ShapeDtypeStruct(out.shape, out.dtype),
            jax.ShapeDtypeStruct((p * q,) + stat.shape, stat.dtype),
        ),
        in_specs=[anyspace] * 2,
        out_specs=(anyspace,) * 2,
        scratch_shapes=[dma((p,)), dma((p,)), dma((p * q,)), dma((p * q,)), dma((2,))],
        compiler_params=pltpu.CompilerParams(collective_id=1, has_side_effects=True),
    )(out, stat)


def apply_kernel(li, ri, pi, ok, rows, cols, psi0, psi1, l0, l1, r0, r1, out_ref, stat_ref):
    s = pl.program_id(0) * 2
    tile = l0.shape[1]
    wide = 4 * tile
    chunks = l0.shape[2] // wide
    live = ok[s] + ok[s + 1]

    @pl.when(live > 0)
    def _():
        ia = lax.broadcasted_iota(jnp.int32, (wide, wide), 0) // tile
        ib = lax.broadcasted_iota(jnp.int32, (wide, wide), 1) // tile
        a = lax.broadcasted_iota(jnp.int32, (tile, tile), 0)
        e = lax.broadcasted_iota(jnp.int32, (tile, tile), 1)
        psis, diags = [], []
        for half, psi_ref in enumerate((psi0, psi1)):
            pair = psi_ref[0].astype(jnp.float32)
            psi_f = jnp.where(pi[s + half] % 2 == 0, pair[:, :tile], pair[:, tile:])
            psi_f = jnp.where(ok[s + half] > 0, psi_f, 0.0)
            psi = psi_f.astype(jnp.bfloat16)
            row = jnp.concatenate([psi] * 4, axis=1)
            full = jnp.concatenate([row] * 4, axis=0)
            psis.append(psi_f)
            diags.append(jnp.where(ia == ib, full, jnp.zeros_like(full)))
        parts = [[], []]
        for k in range(chunks):
            cut = slice(k * wide, (k + 1) * wide)
            for half, l_ref in enumerate((l0, l1)):
                t = jnp.dot(l_ref[0, :, cut], diags[half], preferred_element_type=jnp.float32)
                parts[half].append(t.astype(jnp.bfloat16))
        for half, r_ref in enumerate((r0, r1)):
            lanes = slice(half * tile, (half + 1) * tile)
            t = jnp.concatenate(parts[half], axis=1)
            acc = lax.dot_general(t, r_ref[0], (((1,), (1,)), ((), ())),
                                  preferred_element_type=jnp.float32)
            acc = jnp.where((a < rows[s + half]) & (e < cols[s + half]) & (ok[s + half] > 0), acc, 0.0)
            psi_f = psis[half]
            out_ref[0, :, lanes] = acc
            ph = jnp.sum(psi_f * acc, axis=0, keepdims=True)
            pp = jnp.sum(psi_f * psi_f, axis=0, keepdims=True)
            th = jnp.where(pp > 0, ph / jnp.where(pp > 0, pp, 1.0), 0.0)
            rest = acc - th * psi_f
            stat_ref[0, 0:1, lanes] = ph
            stat_ref[0, 1:2, lanes] = pp
            stat_ref[0, 2:3, lanes] = jnp.sum(rest * rest, axis=0, keepdims=True)
            stat_ref[0, 3:4, lanes] = th

    @pl.when(live == 0)
    def _():
        out_ref[...] = jnp.zeros_like(out_ref)
        stat_ref[...] = jnp.zeros_like(stat_ref)


def apply_blocks(li, ri, pi, ok, rows, cols, psi, left, right):
    pairs = li.shape[0] // 2
    tile = left.shape[1]
    width = left.shape[2]

    def spec(shape, which, half, scale=1):
        return pl.BlockSpec((1,) + shape, lambda j, *ids: (ids[which][2 * j + half] // scale, 0, 0))

    return pl.pallas_call(
        apply_kernel,
        grid_spec=pltpu.PrefetchScalarGridSpec(
            num_scalar_prefetch=6,
            grid=(pairs,),
            in_specs=[
                spec((tile, 2 * tile), 2, 0, 2), spec((tile, 2 * tile), 2, 1, 2),
                spec((tile, width), 0, 0), spec((tile, width), 0, 1),
                spec((tile, width), 1, 0), spec((tile, width), 1, 1),
            ],
            out_specs=[
                pl.BlockSpec((1, tile, 2 * tile), lambda j, *ids: (j, 0, 0)),
                pl.BlockSpec((1, 4, 2 * tile), lambda j, *ids: (j, 0, 0)),
            ],
        ),
        out_shape=[
            jax.ShapeDtypeStruct((pairs, tile, 2 * tile), jnp.float32),
            jax.ShapeDtypeStruct((pairs, 4, 2 * tile), jnp.float32),
        ],
        compiler_params=pltpu.CompilerParams(vmem_limit_bytes=56 * 1024 * 1024),
    )(li, ri, pi, ok, rows, cols, psi, psi, left, left, right, right)


def body(psi_blocks, left_sector, left_dims, right_sector, right_dims, left_env, right_env):
    blocks, tile = psi_blocks.shape[:2]
    left_count = left_env.shape[0]
    right_count = right_env.shape[0]
    owners = lax.axis_size("sector")
    device = lax.axis_index("sector")
    cap = (2 * blocks + owners - 1) // owners
    q = 4
    p = owners // q
    slots = min(q * cap, blocks)
    my_z, my_y = device // q, device % q

    left_local = left_sector - device * left_count
    table = right_sector.reshape(owners, blocks)
    own_sector = lax.dynamic_index_in_dim(table, device, 0, keepdims=False)
    rows = jnp.sum(
        jnp.where(left_local[:, None] == jnp.arange(left_count, dtype=jnp.int32)[None, :],
                  left_dims[None, :], 0), axis=1)
    cols = jnp.sum(
        jnp.where(own_sector[:, None] == jnp.arange(right_dims.shape[0], dtype=jnp.int32)[None, :],
                  right_dims[None, :], 0), axis=1)
    place = jnp.arange(tile, dtype=jnp.int32)
    mask = (place[None, :, None] < rows[:, None, None]) & (
        place[None, None, :] < cols[:, None, None])
    psi_used = jnp.where(mask, psi_blocks, jnp.zeros_like(psi_blocks))
    line = lax.dynamic_index_in_dim(table.reshape(p, q, blocks), my_y, 1, keepdims=False)
    goal = line // (right_count * q)
    order = jnp.arange(blocks, dtype=jnp.int32)
    same = (goal[:, :, None] == goal[:, None, :]) & (order[None, None, :] < order[None, :, None])
    rank = jnp.sum(same.astype(jnp.int32), axis=2)
    half = slots // 2
    own_goal = lax.dynamic_index_in_dim(goal, my_z, 0, keepdims=False)
    own_rank = lax.dynamic_index_in_dim(rank, my_z, 0, keepdims=False)
    spot = jnp.arange(slots, dtype=jnp.int32)
    mine = (own_goal[None, None, :] == jnp.arange(p, dtype=jnp.int32)[:, None, None]) & (
        own_rank[None, None, :] == spot[None, :, None])

    def own_pick(values):
        return jnp.sum(jnp.where(mine, values, 0), axis=2)

    picked = jnp.take(psi_used, own_pick(order).reshape(-1), axis=0)
    picked = picked.reshape(p, half, 2, tile, tile).transpose(0, 1, 3, 2, 4)
    picked = picked.reshape(p, half, tile, 2 * tile)
    extra = jnp.stack([own_pick(left_local), own_pick(rows)], axis=1).astype(jnp.bfloat16)
    extra = jnp.pad(extra, ((0, 0), (0, tile - 2), (0, 2 * tile - slots)))
    sent = jnp.concatenate([picked, extra[:, None]], axis=1)

    left_all, right_all, psi_all = gather(p, q, left_env, right_env, sent)
    notes = psi_all[:, half, :2, :slots].astype(jnp.int32)
    left_all = left_all.reshape(p * left_count, tile, -1)
    right_all = right_all.reshape(q * right_count, tile, -1)
    psi_all = psi_all.reshape(p * (half + 1), tile, 2 * tile)

    match = (goal[:, None, :] == my_z) & (
        rank[:, None, :] == jnp.arange(slots, dtype=jnp.int32)[None, :, None])

    def pick(values):
        return jnp.sum(jnp.where(match, values, 0), axis=2).reshape(p * slots)

    ok = pick(jnp.ones((p, 1, blocks), jnp.int32))
    base = jnp.arange(p, dtype=jnp.int32)[:, None]
    pi = (base * (slots + 2) + spot[None]).reshape(p * slots)
    li = (base * left_count + notes[:, 0]).reshape(p * slots)
    slot_rows = notes[:, 1].reshape(p * slots)
    local_right = line[:, None, :] - my_z * (q * right_count)
    ri = pick(local_right)
    my_dims = lax.dynamic_slice_in_dim(right_dims, my_z * (q * right_count), q * right_count)
    slot_cols = jnp.sum(
        jnp.where(ri[:, None] == jnp.arange(q * right_count, dtype=jnp.int32)[None, :],
                  my_dims[None, :], 0), axis=1)
    out, stat = apply_blocks(li, ri, pi, ok, slot_rows, slot_cols, psi_all, left_all, right_all)
    ph, pp = jnp.sum(stat[:, 0]), jnp.sum(stat[:, 1])
    local = jnp.where(pp > 0, ph / jnp.where(pp > 0, pp, 1.0), 0.0)
    ss = jnp.sum(stat[:, 2] + (stat[:, 3] - local) ** 2 * stat[:, 1])
    stat = jnp.broadcast_to(jnp.pad(jnp.stack([ph, pp, ss, local]), (0, 4))[:, None], (8, 128))
    back, stat_all = give_back(p, q, out.reshape(p, slots // 2, tile, 2 * tile), stat)

    own_rank = lax.dynamic_index_in_dim(rank, my_z, 0, keepdims=False)
    target = (own_sector // (right_count * q)) * slots + own_rank
    got = jnp.take(back.reshape(p * slots // 2, tile, 2 * tile), target // 2, axis=0)
    got = jnp.where((target % 2 == 0)[:, None, None], got[:, :, :tile], got[:, :, tile:])
    hpsi = jnp.where(mask, got, jnp.float32(0.0))

    psi_float = psi_used.astype(jnp.float32)
    stat_all = stat_all[:, :4, 0]
    theta = jnp.sum(stat_all[:, 0]) / jnp.sum(stat_all[:, 1])
    gap = stat_all[:, 3] - theta
    spread = jnp.sum(stat_all[:, 2] + gap * gap * stat_all[:, 1])
    resid = hpsi - theta * psi_float
    scale = jnp.sqrt(spread / (blocks * owners * tile * tile) + 1e-06)
    return (hpsi, resid / scale, jnp.reshape(theta, (1,)))


def solution(mesh):
    placed = (
        P(("groups", "sector"), None, None),
        P(("groups", "sector")),
        P(("groups", "sector")),
        P("groups"),
        P("groups"),
        P(("groups", "sector"), None, None),
        P(("groups", "sector"), None, None),
    )
    return jax.shard_map(
        body,
        mesh=mesh,
        in_specs=placed,
        out_specs=(
            P(("groups", "sector"), None, None),
            P(("groups", "sector"), None, None),
            P("groups"),
        ),
        check_vma=False,
    )
```
